256 devices in a mesh: prompt: 2 (over x_lo), group: 16 (over z, x_hi), tensor: 8 (over y, core).
Axes of the slice: x: 4 (x_hi: 2, x_lo: 2; x = x_hi * 2 + x_lo), y: 4, z: 8, core: 2. Of those that a mesh axis runs over, the one named last changes fastest.
Arguments:
- queries: bfloat16 [32, 512, 4096], P(('prompt', 'group'), None, 'tensor'), parts along dimension 0
- response_kv: bfloat16 [32, 2, 512, 1024], P(('prompt', 'group'), None, None, 'tensor'), parts along dimension 0
- grad_out: bfloat16 [32, 512, 4096], P(('prompt', 'group'), None, 'tensor'), parts along dimension 0, may hold values from -6 to 6
- prefix_kv: bfloat16 [32, 2, 2048, 1024], P(('prompt', 'group'), None, None, 'tensor'), parts along dimension 0, may hold values from -6 to 6
- kv_weight: bfloat16 [2, 5120, 1024], P(None, None, 'tensor'), may hold values from -0.078125 to 0.078125
- resp_len: int32 [32], P(('prompt', 'group')), parts along dimension 0, may hold values from 1 to 512, 4352 in all
- prefix_len: int32 [2], P('prompt'), parts along dimension 0, may hold values from 1024 to 2048
- owner: int32 [2], P('prompt'), parts along dimension 0, may hold values from 0 to 15
Outputs:
- query_grad: bfloat16 [32, 512, 4096], P(('prompt', 'group'), None, 'tensor'), parts along dimension 0
- kv_grad: bfloat16 [32, 2, 512, 1024], P(('prompt', 'group'), None, None, 'tensor'), parts along dimension 0
- input_grad: bfloat16 [4096, 5120], P(('prompt', 'group'), 'tensor'), parts along dimension 0
The draws below stay inside these ranges and needn't reach their ends.
There are 2 independent parts, one for each index of `prompt`. The reference program is written for one: setup_inputs(seed, part) draws one part's arguments, and reference() takes and returns one part's arrays. A program takes and returns all parts, laid end to end along the dimension named above; an argument that names none is the same for every part. Nothing has to cross between parts.
Inputs may be any that keep to these rules, and one draw needn't show every extreme that they name: `resp_len`: each response has 1 to 512 live positions, and some response has exactly 512. `prefix_len`: at least half of the prefix is live. Only the owner's slot of prefix_kv is read.
All inputs are finite; a program needn't handle non-finite values. No bound on the sum of `resp_len` on one device may be relied on, other than what follows from the above.
Results may differ from the reference program's by a relative error of at most 0.015.
Values may be sent and summed in bfloat16 or wider, within the bound.
No kernel may reach another device: no remote copies, remote signals or barrier semaphores. Data moves between devices by JAX's collectives and lax.ppermute only.
A program may use at most 128 MiB of HBM per device.

```python
import math
import jax
import jax.numpy as jnp
import numpy as np
from jax import lax

D = 5120
DH = 128
Q_PER_KV = 4
RLEN = 512
PLEN = 2048
KV_HEADS = 8
QH = 32
RESPONSES = 16
N_GROUP = 16


def shared_keys(key):
    return jax.random.normal(key, (RESPONSES, RLEN, KV_HEADS, DH), jnp.float32)


def draw_queries(key, part):
    key = jax.random.fold_in(key, 1)
    drawn = jax.random.normal(key, (RESPONSES, RLEN, KV_HEADS, Q_PER_KV, DH), jnp.float32)
    return drawn.reshape(RESPONSES, RLEN, KV_HEADS * Q_PER_KV * DH).astype(jnp.bfloat16)


def draw_response_kv(key, part):
    key_base = shared_keys(key)
    key = jax.random.fold_in(key, 2)
    values_drawn = jax.random.normal(key, (RESPONSES, RLEN, KV_HEADS, DH), jnp.float32)
    stacked = jnp.stack([key_base, values_drawn], 1)
    return stacked.reshape(RESPONSES, 2, RLEN, KV_HEADS * DH).astype(jnp.bfloat16)


def block_levels(rng, dims, split, least, high):
    factor_of, own = 1.0, jax.random.fold_in(rng, 6)
    for axis_at, parts in split:
        heights = jnp.exp(jax.random.uniform(jax.random.fold_in(own, axis_at), (parts,), jnp.float32, least / len(split), high / len(split)))
        factor_of = factor_of * jnp.repeat(heights, dims[axis_at] // parts).reshape([-1 if axis == axis_at else 1 for axis in range(len(dims))])
    return factor_of


def split_up(count, total, reach, skew):
    loads = [(1 << 20) // math.isqrt(standing ** skew) + 1 for standing in range(2, count + 1)]
    rest, given = total - reach - (count - 1), [1] * (count - 1)
    while rest > 0:
        candidates = [i for i in range(count - 1) if given[i] < reach]
        pool, budget = sum([loads[i] for i in candidates]), rest
        for i in candidates:
            addition = min(reach - given[i], max(1, budget * loads[i] // pool), rest)
            given[i] = given[i] + addition
            rest = rest - addition
    return np.array([reach] + given)


def uneven(key, amount, total, reach, slope):
    if amount == 2:
        one = jax.random.randint(key, (), max(1, total - reach), min(reach, total - 1) + 1)
        return jnp.stack([one, total - one])
    lengths = jnp.asarray(split_up(amount, total, reach, slope), jnp.int32)
    pairs = (amount - 1) // 2
    source_of, taker = lengths[1:1 + 2 * pairs:2], lengths[2:2 + 2 * pairs:2]
    margin = jnp.minimum(source_of - 1, reach - taker)
    shifted = jax.random.randint(jax.random.fold_in(key, 1), (pairs,), 0, 1 << 20) % (margin + 1)
    lengths = lengths.at[1:1 + 2 * pairs:2].set(source_of - shifted).at[2:2 + 2 * pairs:2].set(taker + shifted)
    return lengths[jax.random.permutation(jax.random.fold_in(key, 2), amount)]


def noise(rng, shape, deviation, bound, cuts=(), dtype=jnp.bfloat16):
    array = deviation * jax.random.normal(rng, shape, jnp.float32)
    if cuts:
        array = array * block_levels(rng, shape, cuts, -0.22, 0.18)
    return jnp.clip(array, -bound, bound).astype(dtype)


def setup_inputs(seed: int = 0, part: int = 0) -> dict:
    seeds = jax.random.split(jax.random.key(seed), 9)
    own_keys = jax.random.split(jax.random.fold_in(seeds[8], part), 9)
    queries = draw_queries(jax.random.fold_in(jax.random.fold_in(seeds[8], part), 71), part)
    response_kv = draw_response_kv(jax.random.fold_in(jax.random.fold_in(seeds[8], part), 71), part)
    grad_out = noise(own_keys[2], (RESPONSES, RLEN, QH * DH), 1.0, 6.0, ((0, 16), (2, 8)))
    prefix_kv = noise(own_keys[3], (N_GROUP, 2, PLEN, KV_HEADS * DH), 1.0, 6.0, ((0, 16), (3, 8)))
    kv_weight = noise(seeds[4], (2, D, KV_HEADS * DH), D ** -0.5, 0.078125, ((2, 8),))
    resp_len = uneven(own_keys[5], RESPONSES, RESPONSES * RLEN // 2 + RLEN // 2, RLEN, 1).astype(jnp.int32)
    prefix_len = jax.random.randint(own_keys[6], (1,), PLEN // 2, PLEN + 1).astype(jnp.int32)
    owner = jax.random.randint(own_keys[7], (1,), 0, N_GROUP).astype(jnp.int32)
    return dict(queries=queries, response_kv=response_kv, grad_out=grad_out, prefix_kv=prefix_kv, kv_weight=kv_weight, resp_len=resp_len, prefix_len=prefix_len, owner=owner)


def reference(queries, response_kv, grad_out, prefix_kv, kv_weight, resp_len, prefix_len, owner):
    scaling = DH ** -0.5
    highest = lax.Precision.HIGHEST
    prefix = lax.dynamic_index_in_dim(prefix_kv, owner[0], 0, keepdims=False)
    key_pos = jnp.arange(PLEN + RLEN)
    row_ids = jnp.arange(RLEN)
    allowed = jnp.where(key_pos[None, :] < PLEN, key_pos[None, :] < prefix_len[0], key_pos[None, :] - PLEN <= row_ids[:, None])

    def per_response(running, sliced):
        own_query, own_pair, own_grad, resp_length = sliced
        all_keys = jnp.concatenate([prefix[0], own_pair[0]], 0).reshape(PLEN + RLEN, KV_HEADS, DH).astype(jnp.float32)
        all_values = jnp.concatenate([prefix[1], own_pair[1]], 0).reshape(PLEN + RLEN, KV_HEADS, DH).astype(jnp.float32)
        query_f = own_query.reshape(RLEN, KV_HEADS, Q_PER_KV, DH).astype(jnp.float32)
        grad_f = own_grad.reshape(RLEN, KV_HEADS, Q_PER_KV, DH).astype(jnp.float32)
        scores = jnp.einsum('igxd,jgd->gxij', query_f, all_keys, precision=highest) * scaling
        scores = jnp.where(allowed, scores, -jnp.inf)
        raised = jnp.exp(scores - jnp.max(scores, -1, keepdims=True))
        probs = raised / jnp.sum(raised, -1, keepdims=True)
        row_live = row_ids < resp_length
        probs = jnp.where(row_live[:, None], probs, jnp.float32(0.0))
        probs_low = lax.optimization_barrier(probs.astype(jnp.bfloat16)).astype(jnp.float32)
        attended = jnp.einsum('gxij,jgd->igxd', probs_low, all_values, precision=highest)
        row_dot = jnp.transpose(jnp.sum(grad_f * attended, -1), (1, 2, 0))
        grad_probs = jnp.einsum('igxd,jgd->gxij', grad_f, all_values, precision=highest)
        grad_scores = probs * (grad_probs - row_dot[..., None])
        scores_low = lax.optimization_barrier(grad_scores.astype(jnp.bfloat16)).astype(jnp.float32)
        query_grad = jnp.einsum('gxij,jgd->igxd', scores_low, all_keys, precision=highest) * scaling
        key_grad = jnp.einsum('gxij,igxd->jgd', scores_low, query_f, precision=highest) * scaling
        value_grad = jnp.einsum('gxij,igxd->jgd', probs_low, grad_f, precision=highest)
        own_kv = jnp.stack([key_grad[PLEN:], value_grad[PLEN:]]).reshape(2, RLEN, KV_HEADS * DH).astype(jnp.bfloat16)
        running = running + jnp.stack([key_grad[:PLEN], value_grad[:PLEN]]).reshape(2, PLEN, KV_HEADS * DH)
        return running, (query_grad.reshape(RLEN, QH * DH).astype(jnp.bfloat16), own_kv)

    start_sum = jnp.zeros((2, PLEN, KV_HEADS * DH), jnp.float32)
    running, outputs = lax.scan(per_response, start_sum, (queries, response_kv, grad_out, resp_len))
    key_proj = kv_weight[0].astype(jnp.float32)
    value_proj = kv_weight[1].astype(jnp.float32)
    input_grad = jnp.dot(running[0], key_proj.T, precision=highest) + jnp.dot(running[1], value_proj.T, precision=highest)
    return outputs[0], outputs[1], input_grad.astype(jnp.bfloat16)
```

```python
import functools

import jax
import jax.numpy as jnp
from jax import lax
from jax.experimental import pallas as pl
from jax.experimental.pallas import tpu as pltpu
from jax.sharding import PartitionSpec as P

LAST = (((1,), (1,)), ((), ()))
PLAIN = (((1,), (0,)), ((), ()))
LOG2E = 1.4426950408889634
SPLIT = 8

def dot(a, b, dims=PLAIN):
    return lax.dot_general(a, b, dims, preferred_element_type=jnp.float32)


def block_scores(kind, keys, q, scal_ref, scale2):
    s = dot(keys, q, LAST) * scale2
    at = lax.broadcasted_iota(jnp.int32, s.shape, 0)
    if kind is None:
        ok = at <= lax.broadcasted_iota(jnp.int32, s.shape, 1)
    else:
        base = lax.rem(scal_ref[2] + kind, SPLIT) * s.shape[0]
        ok = at < scal_ref[0] - base
    return jnp.where(ok, s, -jnp.inf)


def forward_kernel(kinds, scale2, first, last, scal_ref, q_ref, g_ref, *refs):
    n = len(kinds)
    kv = refs[:n]
    if first:
        out_ref = refs[n]
    else:
        in_ref, out_ref = refs[n:n + 2]
    q = q_ref[...]
    g = g_ref[...]
    if first:
        m = l = r = None
    else:
        m, l, r = in_ref[0, 0:1], in_ref[0, 1:2], in_ref[0, 2:3]
    for kind, ref in zip(kinds, kv):
        s = block_scores(kind, ref[0], q, scal_ref, scale2)
        top = jnp.max(s, 0, keepdims=True)
        new = top if m is None else jnp.maximum(m, top)
        p = jnp.exp2(s - new)
        dp = dot(ref[1], g, LAST)
        lb = jnp.sum(p, 0, keepdims=True)
        rb = jnp.sum(p * dp, 0, keepdims=True)
        if m is None:
            l, r = lb, rb
        else:
            a = jnp.exp2(m - new)
            l, r = l * a + lb, r * a + rb
        m = new
    if last:
        live = lax.broadcasted_iota(jnp.int32, m.shape, 1) < scal_ref[1]
        m = jnp.where(live, m + jnp.log2(l), jnp.inf)
        r = r / l
    out_ref[0, 0:1] = m
    out_ref[0, 1:2] = l
    out_ref[0, 2:3] = r


def forward(scal, q, g, kinds, blocks, stats, scale2, last):
    rows, width = q.shape
    dh = blocks[0].shape[2]
    heads = width // dh
    first = stats is None
    col = pl.BlockSpec((rows, dh), lambda h: (0, h))
    stat = pl.BlockSpec((1, 8, rows), lambda h: (h, 0, 0))
    full = [pl.BlockSpec(b.shape, lambda h: (0, 0, 0)) for b in blocks]
    keys = sum(b.shape[1] for b in blocks)
    return pl.pallas_call(
        functools.partial(forward_kernel, kinds, scale2, first, last),
        grid=(heads,),
        in_specs=[pl.BlockSpec(memory_space=pltpu.SMEM), col, col] + full + ([] if first else [stat]),
        out_specs=stat,
        out_shape=jax.ShapeDtypeStruct((heads, 8, rows), jnp.float32),
        cost_estimate=pl.CostEstimate(flops=4 * heads * rows * keys * dh, bytes_accessed=4 * q.size, transcendentals=heads * rows * keys),
        compiler_params=pltpu.CompilerParams(vmem_limit_bytes=48 * 2**20),
    )(scal, q, g, *blocks, *([] if first else [stats]))


def backward_kernel(kinds, scale, scale2, first, last, heads, scal_ref, q_ref, g_ref, stat_ref, *refs):
    n = len(kinds)
    kv, refs = refs[:n], refs[n:]
    if not first:
        dq_in, refs = refs[0], refs[1:]
    dq_ref, outs, accs = refs[0], refs[1:1 + n], refs[1 + n:]
    h = pl.program_id(0)
    q = q_ref[...]
    g = g_ref[...]
    mm = stat_ref[0, 0:1]
    rr = stat_ref[0, 2:3]
    dqt = None if first else dq_in[...]
    for kind, ref, out, acc in zip(kinds, kv, outs, accs):
        keys = ref[0]
        s = block_scores(kind, keys, q, scal_ref, scale2)
        p = jnp.exp2(s - mm)
        dp = dot(ref[1], g, LAST)
        ds = (p * (dp - rr)).astype(jnp.bfloat16)
        pb = p.astype(jnp.bfloat16)
        dv = dot(pb, g)
        dk = dot(ds, q)

        @pl.when(h == 0)
        def _():
            acc[0] = dk
            acc[1] = dv

        @pl.when(h != 0)
        def _():
            acc[0] += dk
            acc[1] += dv
        part = dot(keys.T, ds)
        dqt = part if dqt is None else dqt + part
    if last:
        dq_ref[...] = (dqt.T * scale).astype(dq_ref.dtype)
    else:
        dq_ref[...] = dqt

    @pl.when(h == heads - 1)
    def _():
        for out, acc in zip(outs, accs):
            out[0] = (acc[0] * scale).astype(out.dtype)
            out[1] = acc[1].astype(out.dtype)


def backward(scal, q, g, stats, kinds, blocks, dq, scale, scale2, last):
    rows, width = q.shape
    dh = blocks[0].shape[2]
    heads = width // dh
    first = dq is None
    col = pl.BlockSpec((rows, dh), lambda h: (0, h))
    stat = pl.BlockSpec((1, 8, rows), lambda h: (h, 0, 0))
    full = [pl.BlockSpec(b.shape, lambda h: (0, 0, 0)) for b in blocks]
    tall = pl.BlockSpec((dh, rows), lambda h: (h, 0))
    keys = sum(b.shape[1] for b in blocks)
    if last:
        dq_shape, dq_spec = jax.ShapeDtypeStruct((rows, width), jnp.bfloat16), col
    else:
        dq_shape, dq_spec = jax.ShapeDtypeStruct((width, rows), jnp.float32), tall
    res = pl.pallas_call(
        functools.partial(backward_kernel, kinds, scale, scale2, first, last, heads),
        grid=(heads,),
        in_specs=[pl.BlockSpec(memory_space=pltpu.SMEM), col, col, stat] + full + ([] if first else [tall]),
        out_specs=[dq_spec] + full,
        out_shape=[dq_shape] + [jax.ShapeDtypeStruct(b.shape, jnp.bfloat16) for b in blocks],
        scratch_shapes=[pltpu.VMEM(b.shape, jnp.float32) for b in blocks],
        cost_estimate=pl.CostEstimate(flops=10 * heads * rows * keys * dh, bytes_accessed=4 * q.size, transcendentals=heads * rows * keys),
        compiler_params=pltpu.CompilerParams(vmem_limit_bytes=48 * 2**20),
    )(scal, q, g, stats, *blocks, *([] if first else [dq]))
    return res[0], list(res[1:])


def ring(size, step, stride):
    block = size // stride * stride
    return [(i, (i // stride + step) * stride % block + i % stride) for i in range(size)]


def swap(size):
    return [(i, i ^ 1) for i in range(size)]


def z_hop(x, step):
    return lax.ppermute(x, "group", ring(2 * SPLIT, step, 2))


def x_swap(x):
    return lax.ppermute(x, "group", swap(2 * SPLIT))


def scatter_prefix(prefix, z, owner_z):
    keys = prefix.shape[1] // SPLIT
    is_owner = z == owner_z

    def piece(step):
        return lax.dynamic_slice_in_dim(prefix, lax.rem(z + step + SPLIT, SPLIT) * keys, keys, 1)

    up = down = None
    for left in range(SPLIT // 2, 0, -1):
        own = piece(left)
        up = z_hop(own if up is None else jnp.where(is_owner, own, up), 1)
        if left < SPLIT // 2:
            own = piece(-left)
            down = z_hop(own if down is None else jnp.where(is_owner, own, down), -1)
    away = lax.rem(z - owner_z + SPLIT, SPLIT)
    return jnp.where(is_owner, piece(0), jnp.where(away <= SPLIT // 2, up, down))


def add_low(a, b):
    return (a.astype(jnp.float32) + b.astype(jnp.float32)).astype(jnp.bfloat16)


def on_device(queries, response_kv, grad_out, prefix_kv, kv_weight, resp_len, prefix_len, owner):
    group = lax.axis_index("group")
    tensor = lax.axis_index("tensor")
    z, x, core, y = group // 2, group % 2, tensor % 2, tensor // 2
    dh = prefix_kv.shape[3]
    scale = dh ** (-0.5)
    scale2 = scale * LOG2E
    q, g, own = queries[0], grad_out[0], response_kv[0]
    scal = jnp.stack([prefix_len[0], resp_len[0], z, z]).astype(jnp.int32)

    cols = kv_weight.shape[1] // 8
    by_core = kv_weight.reshape(2, 4, 2, cols, dh)
    mine = lax.dynamic_index_in_dim(by_core, core, 2, keepdims=False)
    other = lax.ppermute(lax.dynamic_index_in_dim(by_core, 1 - core, 2, keepdims=False), "tensor", swap(8))

    stats = forward(scal, q, g, (None,), [own], None, scale2, False)

    piece = scatter_prefix(prefix_kv[0], z, owner[0] // 2)
    piece = jnp.where(x == owner[0] % 2, piece, x_swap(piece))

    pieces = {0: piece}
    stats = forward(scal, q, g, (0,), [piece], stats, scale2, False)
    up = down = piece
    for hop in range(1, SPLIT // 2 + 1):
        up = z_hop(up, 1)
        pieces[SPLIT - hop] = up
        new = [SPLIT - hop]
        if hop < SPLIT // 2:
            down = z_hop(down, -1)
            pieces[hop] = down
            new.append(hop)
        stats = forward(scal, q, g, tuple(new), [pieces[k] for k in new], stats, scale2, hop == SPLIT // 2)

    dq = up = down = None
    for left in range(SPLIT // 2, 0, -1):
        new = [left] if left == SPLIT // 2 else [left, SPLIT - left]
        dq, grads = backward(scal, q, g, stats, tuple(new), [pieces[k] for k in new], dq, scale, scale2, False)
        up = z_hop(grads[0] if up is None else add_low(grads[0], up), 1)
        if len(new) > 1:
            down = z_hop(grads[1] if down is None else add_low(grads[1], down), -1)
    dq, (last,) = backward(scal, q, g, stats, (0,), [pieces[0]], dq, scale, scale2, False)
    total = last.astype(jnp.float32) + up.astype(jnp.float32) + down.astype(jnp.float32)
    half = total.shape[1] // 2
    keep = lax.dynamic_slice_in_dim(total, x * half, half, 1)
    send = lax.dynamic_slice_in_dim(total, (1 - x) * half, half, 1).astype(jnp.bfloat16)
    summed = (keep + x_swap(send).astype(jnp.float32)).astype(jnp.bfloat16)
    dq, (own_grad,) = backward(scal, q, g, stats, (None,), [own], dq, scale, scale2, True)

    beside = lax.ppermute(summed, "tensor", swap(8))
    rows = jnp.concatenate([summed[0], summed[1], beside[0], beside[1]], 1)
    weights = jnp.concatenate([mine[0], mine[1], other[0], other[1]], 2)
    shares = lax.dot_general(
        rows, weights.reshape(4 * cols, 4 * dh), LAST, preferred_element_type=jnp.float32
    ).astype(jnp.bfloat16)

    def share(k):
        return lax.dynamic_slice_in_dim(shares, lax.rem(y + k, 4) * cols, cols, 1)

    result = share(0).astype(jnp.float32)
    for k in (1, 2, 3):
        result = result + lax.ppermute(share(k), "tensor", ring(8, k, 2)).astype(jnp.float32)
    return dq[None], own_grad[None], result.astype(jnp.bfloat16)


def solution(mesh):
    in_specs = (
        P(("prompt", "group"), None, "tensor"),
        P(("prompt", "group"), None, None, "tensor"),
        P(("prompt", "group"), None, "tensor"),
        P(("prompt", "group"), None, None, "tensor"),
        P(None, None, "tensor"),
        P(("prompt", "group")),
        P("prompt"),
        P("prompt"),
    )
    out_specs = (
        P(("prompt", "group"), None, "tensor"),
        P(("prompt", "group"), None, None, "tensor"),
        P(("prompt", "group"), "tensor"),
    )
    return jax.shard_map(
        on_device, mesh=mesh, in_specs=in_specs, out_specs=out_specs, check_vma=False
    )
```

```python
import functools

import jax
import jax.numpy as jnp
from jax import lax
from jax.experimental import pallas as pl
from jax.experimental.pallas import tpu as pltpu
from jax.sharding import PartitionSpec as P

LAST = (((1,), (1,)), ((), ()))
PLAIN = (((1,), (0,)), ((), ()))
LOG2E = 1.4426950408889634
SPLIT = 8

def dot(a, b, dims=PLAIN):
    return lax.dot_general(a, b, dims, preferred_element_type=jnp.float32)


def block_scores(kind, keys, q, scal_ref, scale2):
    s = dot(keys, q, LAST) * scale2
    at = lax.broadcasted_iota(jnp.int32, s.shape, 0)
    if kind is None:
        ok = at <= lax.broadcasted_iota(jnp.int32, s.shape, 1)
    else:
        base = lax.rem(scal_ref[2] + kind, SPLIT) * s.shape[0]
        ok = at < scal_ref[0] - base
    return jnp.where(ok, s, -jnp.inf)


def forward_kernel(kinds, scale2, first, last, scal_ref, q_ref, g_ref, *refs):
    n = len(kinds)
    kv = refs[:n]
    if first:
        out_ref = refs[n]
    else:
        in_ref, out_ref = refs[n:n + 2]
    q = q_ref[...]
    g = g_ref[...]
    if first:
        m = l = r = None
    else:
        m, l, r = in_ref[0, 0:1], in_ref[0, 1:2], in_ref[0, 2:3]
    for kind, ref in zip(kinds, kv):
        s = block_scores(kind, ref[0], q, scal_ref, scale2)
        top = jnp.max(s, 0, keepdims=True)
        new = top if m is None else jnp.maximum(m, top)
        p = jnp.exp2(s - new)
        dp = dot(ref[1], g, LAST)
        lb = jnp.sum(p, 0, keepdims=True)
        rb = jnp.sum(p * dp, 0, keepdims=True)
        if m is None:
            l, r = lb, rb
        else:
            a = jnp.exp2(m - new)
            l, r = l * a + lb, r * a + rb
        m = new
    if last:
        live = lax.broadcasted_iota(jnp.int32, m.shape, 1) < scal_ref[1]
        m = jnp.where(live, m + jnp.log2(l), jnp.inf)
        r = r / l
    out_ref[0, 0:1] = m
    out_ref[0, 1:2] = l
    out_ref[0, 2:3] = r


def forward(scal, q, g, kinds, blocks, stats, scale2, last):
    rows, width = q.shape
    dh = blocks[0].shape[2]
    heads = width // dh
    first = stats is None
    col = pl.BlockSpec((rows, dh), lambda h: (0, h))
    stat = pl.BlockSpec((1, 8, rows), lambda h: (h, 0, 0))
    full = [pl.BlockSpec(b.shape, lambda h: (0, 0, 0)) for b in blocks]
    keys = sum(b.shape[1] for b in blocks)
    return pl.pallas_call(
        functools.partial(forward_kernel, kinds, scale2, first, last),
        grid=(heads,),
        in_specs=[pl.BlockSpec(memory_space=pltpu.SMEM), col, col] + full + ([] if first else [stat]),
        out_specs=stat,
        out_shape=jax.ShapeDtypeStruct((heads, 8, rows), jnp.float32),
        cost_estimate=pl.CostEstimate(flops=4 * heads * rows * keys * dh, bytes_accessed=4 * q.size, transcendentals=heads * rows * keys),
        compiler_params=pltpu.CompilerParams(vmem_limit_bytes=48 * 2**20),
    )(scal, q, g, *blocks, *([] if first else [stats]))


def backward_kernel(kinds, scale, scale2, first, last, heads, scal_ref, q_ref, g_ref, stat_ref, *refs):
    n = len(kinds)
    kv, refs = refs[:n], refs[n:]
    if not first:
        dq_in, refs = refs[0], refs[1:]
    dq_ref, outs, accs = refs[0], refs[1:1 + n], refs[1 + n:]
    h = pl.program_id(0)
    q = q_ref[...]
    g = g_ref[...]
    mm = stat_ref[0, 0:1]
    rr = stat_ref[0, 2:3]
    dqt = None if first else dq_in[...]
    for kind, ref, out, acc in zip(kinds, kv, outs, accs):
        keys = ref[0]
        s = block_scores(kind, keys, q, scal_ref, scale2)
        p = jnp.exp2(s - mm)
        dp = dot(ref[1], g, LAST)
        ds = (p * (dp - rr)).astype(jnp.bfloat16)
        pb = p.astype(jnp.bfloat16)
        dv = dot(pb, g)
        dk = dot(ds, q)

        @pl.when(h == 0)
        def _():
            acc[0] = dk
            acc[1] = dv

        @pl.when(h != 0)
        def _():
            acc[0] += dk
            acc[1] += dv
        part = dot(keys.T, ds)
        dqt = part if dqt is None else dqt + part
    if last:
        dq_ref[...] = (dqt.T * scale).astype(dq_ref.dtype)
    else:
        dq_ref[...] = dqt

    @pl.when(h == heads - 1)
    def _():
        for out, acc in zip(outs, accs):
            out[0] = (acc[0] * scale).astype(out.dtype)
            out[1] = acc[1].astype(out.dtype)


def backward(scal, q, g, stats, kinds, blocks, dq, scale, scale2, last):
    rows, width = q.shape
    dh = blocks[0].shape[2]
    heads = width // dh
    first = dq is None
    col = pl.BlockSpec((rows, dh), lambda h: (0, h))
    stat = pl.BlockSpec((1, 8, rows), lambda h: (h, 0, 0))
    full = [pl.BlockSpec(b.shape, lambda h: (0, 0, 0)) for b in blocks]
    tall = pl.BlockSpec((dh, rows), lambda h: (h, 0))
    keys = sum(b.shape[1] for b in blocks)
    if last:
        dq_shape, dq_spec = jax.ShapeDtypeStruct((rows, width), jnp.bfloat16), col
    else:
        dq_shape, dq_spec = jax.ShapeDtypeStruct((width, rows), jnp.float32), tall
    res = pl.pallas_call(
        functools.partial(backward_kernel, kinds, scale, scale2, first, last, heads),
        grid=(heads,),
        in_specs=[pl.BlockSpec(memory_space=pltpu.SMEM), col, col, stat] + full + ([] if first else [tall]),
        out_specs=[dq_spec] + full,
        out_shape=[dq_shape] + [jax.ShapeDtypeStruct(b.shape, jnp.bfloat16) for b in blocks],
        scratch_shapes=[pltpu.VMEM(b.shape, jnp.float32) for b in blocks],
        cost_estimate=pl.CostEstimate(flops=10 * heads * rows * keys * dh, bytes_accessed=4 * q.size, transcendentals=heads * rows * keys),
        compiler_params=pltpu.CompilerParams(vmem_limit_bytes=48 * 2**20),
    )(scal, q, g, stats, *blocks, *([] if first else [dq]))
    return res[0], list(res[1:])


def ring(size, step, stride):
    block = size // stride * stride
    return [(i, (i // stride + step) * stride % block + i % stride) for i in range(size)]


def swap(size):
    return [(i, i ^ 1) for i in range(size)]


def z_hop(x, step):
    return lax.ppermute(x, "group", ring(2 * SPLIT, step, 2))


def x_swap(x):
    return lax.ppermute(x, "group", swap(2 * SPLIT))


def after(value, *done):
    return lax.optimization_barrier((value, *done))[0]


def add_low(a, b):
    return (a.astype(jnp.float32) + b.astype(jnp.float32)).astype(jnp.bfloat16)


def on_device(queries, response_kv, grad_out, prefix_kv, kv_weight, resp_len, prefix_len, owner):
    group = lax.axis_index("group")
    tensor = lax.axis_index("tensor")
    z, x, core, y = group // 2, group % 2, tensor % 2, tensor // 2
    dh = prefix_kv.shape[3]
    scale = dh ** (-0.5)
    scale2 = scale * LOG2E
    q, g, own, prefix = queries[0], grad_out[0], response_kv[0], prefix_kv[0]
    scal = jnp.stack([prefix_len[0], resp_len[0], z, z]).astype(jnp.int32)

    keys = prefix.shape[1] // SPLIT
    half_way = SPLIT // 2
    owner_z = owner[0] // 2
    is_owner = z == owner_z
    first = lax.dynamic_slice_in_dim(prefix, lax.rem(z + half_way, SPLIT) * keys, keys, 1)
    turned = lax.dynamic_slice_in_dim(jnp.concatenate([prefix, prefix], 1), z * keys, SPLIT * keys, 1)
    turned = after(turned)

    def piece(step):
        return lax.slice_in_dim(turned, step % SPLIT * keys, (step % SPLIT + 1) * keys, axis=1)

    cols = kv_weight.shape[1] // 8
    by_core = kv_weight.reshape(2, 4, 2, cols, dh)
    mine = lax.dynamic_index_in_dim(by_core, core, 2, keepdims=False)
    theirs = lax.dynamic_index_in_dim(by_core, 1 - core, 2, keepdims=False)

    up = z_hop(first, 1)
    down = z_hop(piece(1 - half_way), -1)
    theirs = after(theirs, turned)
    up, down, theirs, mine = lax.optimization_barrier((up, down, theirs, mine))
    other = lax.ppermute(theirs, "tensor", swap(8))
    up = z_hop(jnp.where(is_owner, piece(half_way - 1), up), 1)
    down = z_hop(jnp.where(is_owner, piece(2 - half_way), down), -1)
    up, down, other = lax.optimization_barrier((up, down, other))
    weights = jnp.concatenate([mine[0], mine[1], other[0], other[1]], 2).reshape(4 * cols, 4 * dh)
    up = z_hop(jnp.where(is_owner, piece(half_way - 2), up), 1)
    down = z_hop(jnp.where(is_owner, piece(3 - half_way), down), -1)
    up, weights = lax.optimization_barrier((up, weights))
    up = z_hop(jnp.where(is_owner, piece(half_way - 3), up), 1)
    stats = forward(scal, q, g, (None,), [own], None, scale2, False)
    up, stats = lax.optimization_barrier((up, stats))
    away = lax.rem(z - owner_z + SPLIT, SPLIT)
    held = jnp.where(is_owner, piece(0), jnp.where(away <= half_way, up, down))
    held = jnp.where(x == owner[0] % 2, held, x_swap(held))

    pieces = {0: held}
    new = [0]
    up = down = held
    for hop in range(1, half_way + 1):
        up = z_hop(up, 1)
        if hop < half_way:
            down = z_hop(down, -1)
        stats = forward(scal, q, g, tuple(new), [pieces[k] for k in new], stats, scale2, False)
        new = [SPLIT - hop]
        if hop < half_way:
            up, down, stats = lax.optimization_barrier((up, down, stats))
            pieces[hop] = down
            new.append(hop)
        else:
            up, stats = lax.optimization_barrier((up, stats))
        pieces[SPLIT - hop] = up
    stats = forward(scal, q, g, tuple(new), [pieces[k] for k in new], stats, scale2, True)

    dq, (grad,) = backward(scal, q, g, stats, (half_way,), [pieces[half_way]], None, scale, scale2, False)
    up, down = z_hop(grad, 1), None
    for left in range(half_way - 1, 0, -1):
        new = (left, SPLIT - left)
        dq, grads = backward(scal, q, g, stats, new, [pieces[k] for k in new], dq, scale, scale2, False)
        up, dq, *grads = lax.optimization_barrier((up, dq, *grads))
        up = z_hop(add_low(grads[0], up), 1)
        down = z_hop(grads[1] if down is None else add_low(grads[1], down), -1)
    dq, (grad,) = backward(scal, q, g, stats, (0,), [pieces[0]], dq, scale, scale2, False)
    up, down, dq, grad = lax.optimization_barrier((up, down, dq, grad))
    half = keys // 2

    def rows_of(at):
        up_, down_, grad_ = (lax.dynamic_slice_in_dim(v, at * half, half, 1).astype(jnp.float32) for v in (up, down, grad))
        return up_ + down_ + grad_

    swapped = x_swap(rows_of(1 - x).astype(jnp.bfloat16))
    dq, (own_grad,) = backward(scal, q, g, stats, (None,), [own], dq, scale, scale2, True)
    swapped, dq, own_grad = lax.optimization_barrier((swapped, dq, own_grad))
    summed = (rows_of(x) + swapped.astype(jnp.float32)).astype(jnp.bfloat16)

    beside = lax.ppermute(summed, "tensor", swap(8))
    rows = jnp.concatenate([summed[0], summed[1], beside[0], beside[1]], 1)
    shares = lax.dot_general(rows, weights, LAST, preferred_element_type=jnp.float32).astype(jnp.bfloat16)

    def share(k):
        return lax.dynamic_slice_in_dim(shares, lax.rem(y + k, 4) * cols, cols, 1)

    result = share(0).astype(jnp.float32)
    for k in (1, 2, 3):
        result = result + lax.ppermute(share(k), "tensor", ring(8, k, 2)).astype(jnp.float32)
    return dq[None], own_grad[None], result.astype(jnp.bfloat16)


def solution(mesh):
    in_specs = (
        P(("prompt", "group"), None, "tensor"),
        P(("prompt", "group"), None, None, "tensor"),
        P(("prompt", "group"), None, "tensor"),
        P(("prompt", "group"), None, None, "tensor"),
        P(None, None, "tensor"),
        P(("prompt", "group")),
        P("prompt"),
        P("prompt"),
    )
    out_specs = (
        P(("prompt", "group"), None, "tensor"),
        P(("prompt", "group"), None, None, "tensor"),
        P(("prompt", "group"), "tensor"),
    )
    return jax.shard_map(
        on_device, mesh=mesh, in_specs=in_specs, out_specs=out_specs, check_vma=False
    )
```

```python
import functools

import jax
import jax.numpy as jnp
from jax import lax
from jax.experimental import pallas as pl
from jax.experimental.pallas import tpu as pltpu
from jax.sharding import PartitionSpec as P

LAST = (((1,), (1,)), ((), ()))
PLAIN = (((1,), (0,)), ((), ()))
LOG2E = 1.4426950408889634
SPLIT = 8
SMEM = pl.BlockSpec(memory_space=pltpu.SMEM)
VMEM = pl.BlockSpec(memory_space=pltpu.VMEM)
ANY = pl.BlockSpec(memory_space=pl.ANY)


def dot(a, b, dims=PLAIN):
    return lax.dot_general(a, b, dims, preferred_element_type=jnp.float32)


def block_scores(kind, keys, q, live_ref, scale2):
    s = dot(keys, q, LAST) * scale2
    at = lax.broadcasted_iota(jnp.int32, s.shape, 0)
    if kind is None:
        ok = at <= lax.broadcasted_iota(jnp.int32, s.shape, 1)
    else:
        base = lax.rem(lax.axis_index("group") // 2 + kind, SPLIT) * s.shape[0]
        ok = at < live_ref[0] - base
    return jnp.where(ok, s, -jnp.inf)


def forward_kernel(kinds, scale2, first, last, heads, live_ref, rows_ref, q_ref, g_ref, *refs):
    n = len(kinds)
    kv = refs[:n]
    out_ref = refs[-1]
    dh = q_ref.shape[1] // heads
    for h in range(heads):
        q = q_ref[:, h * dh:(h + 1) * dh]
        g = g_ref[:, h * dh:(h + 1) * dh]
        if first:
            m = l = r = None
        else:
            m, l, r = refs[n][h, 0:1], refs[n][h, 1:2], refs[n][h, 2:3]
        for kind, ref in zip(kinds, kv):
            s = block_scores(kind, ref[0], q, live_ref, scale2)
            top = jnp.max(s, 0, keepdims=True)
            new = top if m is None else jnp.maximum(m, top)
            p = jnp.exp2(s - new)
            dp = dot(ref[1], g, LAST)
            lb = jnp.sum(p, 0, keepdims=True)
            rb = jnp.sum(p * dp, 0, keepdims=True)
            if m is None:
                l, r = lb, rb
            else:
                a = jnp.exp2(m - new)
                l, r = l * a + lb, r * a + rb
            m = new
        if last:
            live = lax.broadcasted_iota(jnp.int32, m.shape, 1) < rows_ref[0]
            m = jnp.where(live, m + jnp.log2(l), jnp.inf)
            r = r / l
        out_ref[h, 0:1] = m
        out_ref[h, 1:2] = l
        out_ref[h, 2:3] = r


def forward(lens, q, g, kinds, blocks, stats, scale2, last):
    rows, width = q.shape
    dh = blocks[0].shape[2]
    heads = width // dh
    first = stats is None
    keys = sum(b.shape[1] for b in blocks)
    n = 2 + len(blocks) + (not first)
    return pl.pallas_call(
        functools.partial(forward_kernel, kinds, scale2, first, last, heads),
        in_specs=[SMEM] * 2 + [VMEM] * n,
        out_specs=VMEM,
        out_shape=jax.ShapeDtypeStruct((heads, 8, rows), jnp.float32),
        cost_estimate=pl.CostEstimate(flops=4 * heads * rows * keys * dh, bytes_accessed=4 * q.size, transcendentals=heads * rows * keys),
        compiler_params=pltpu.CompilerParams(vmem_limit_bytes=24 * 2**20),
    )(*lens, q, g, *blocks, *([] if first else [stats]))


def backward_kernel(kinds, scale, scale2, first, last, heads, live_ref, rows_ref, q_ref, g_ref, stat_ref, *refs):
    n = len(kinds)
    kv, refs = refs[:n], refs[n:]
    if not first:
        dq_in, refs = refs[0], refs[1:]
    dq_ref, outs, accs = refs[0], refs[1:1 + n], refs[1 + n:]
    dh = q_ref.shape[1] // heads
    for h in range(heads):
        cols = slice(h * dh, (h + 1) * dh)
        q = q_ref[:, cols]
        g = g_ref[:, cols]
        mm = stat_ref[h, 0:1]
        rr = stat_ref[h, 2:3]
        dqt = None if first else dq_in[cols, :]
        for kind, ref, out, acc in zip(kinds, kv, outs, accs):
            keys = ref[0]
            s = block_scores(kind, keys, q, live_ref, scale2)
            p = jnp.exp2(s - mm)
            dp = dot(ref[1], g, LAST)
            ds = (p * (dp - rr)).astype(jnp.bfloat16)
            pb = p.astype(jnp.bfloat16)
            dv = dot(pb, g)
            dk = dot(ds, q)
            if h:
                dk, dv = acc[0] + dk, acc[1] + dv
            if h < heads - 1:
                acc[0] = dk
                acc[1] = dv
            else:
                out[0] = (dk * scale).astype(out.dtype)
                out[1] = dv.astype(out.dtype)
            part = dot(keys.T, ds)
            dqt = part if dqt is None else dqt + part
        if last:
            dq_ref[:, cols] = (dqt.T * scale).astype(dq_ref.dtype)
        else:
            dq_ref[cols, :] = dqt


def backward(lens, q, g, stats, kinds, blocks, dq, scale, scale2, last):
    rows, width = q.shape
    dh = blocks[0].shape[2]
    heads = width // dh
    first = dq is None
    keys = sum(b.shape[1] for b in blocks)
    if last:
        dq_shape = jax.ShapeDtypeStruct((rows, width), jnp.bfloat16)
    else:
        dq_shape = jax.ShapeDtypeStruct((width, rows), jnp.float32)
    n = 3 + len(blocks) + (not first)
    res = pl.pallas_call(
        functools.partial(backward_kernel, kinds, scale, scale2, first, last, heads),
        in_specs=[SMEM] * 2 + [VMEM] * n,
        out_specs=[VMEM] * (1 + len(blocks)),
        out_shape=[dq_shape] + [jax.ShapeDtypeStruct(b.shape, jnp.bfloat16) for b in blocks],
        scratch_shapes=[pltpu.VMEM(b.shape, jnp.float32) for b in blocks],
        cost_estimate=pl.CostEstimate(flops=10 * heads * rows * keys * dh, bytes_accessed=4 * q.size, transcendentals=heads * rows * keys),
        compiler_params=pltpu.CompilerParams(vmem_limit_bytes=24 * 2**20),
    )(*lens, q, g, stats, *blocks, *([] if first else [dq]))
    return res[0], list(res[1:])


def cut_kernel(keys, prefix_ref, *refs):
    outs, sems = refs[:SPLIT], refs[SPLIT]
    z = lax.axis_index("group") // 2
    copies = []
    for step in (4, 3, 5, 2, 6, 1, 7, 0):
        at = pl.multiple_of(lax.rem(z + step, SPLIT) * keys, keys)
        copies.append(pltpu.make_async_copy(prefix_ref.at[:, pl.ds(at, keys), :], outs[step], sems.at[step]))
        copies[-1].start()
    for copy in copies:
        copy.wait()


def cut(prefix, keys):
    shape = (prefix.shape[0], keys, prefix.shape[2])
    return pl.pallas_call(
        functools.partial(cut_kernel, keys),
        in_specs=[ANY],
        out_specs=[ANY] * SPLIT,
        out_shape=[jax.ShapeDtypeStruct(shape, prefix.dtype)] * SPLIT,
        scratch_shapes=[pltpu.SemaphoreType.DMA((SPLIT,))],
    )(prefix)


def lend_kernel(weight_ref, out_ref, sem):
    core = lax.rem(lax.axis_index("tensor"), 2)
    copy = pltpu.make_async_copy(weight_ref.at[:, :, 1 - core], out_ref, sem)
    copy.start()
    copy.wait()


def lend(by_core):
    shape = by_core.shape[:2] + by_core.shape[3:]
    return pl.pallas_call(
        lend_kernel,
        in_specs=[ANY],
        out_specs=VMEM,
        out_shape=jax.ShapeDtypeStruct(shape, by_core.dtype),
        scratch_shapes=[pltpu.SemaphoreType.DMA],
    )(by_core)


def project_kernel(summed_ref, beside_ref, weight_ref, other_ref, out_ref):
    tensor = lax.axis_index("tensor")
    y, core = tensor // 2, lax.rem(tensor, 2)
    for step in range(4):
        at = lax.rem(y + step, 4)
        acc = None
        for j in range(2):
            for rows, block in ((summed_ref[j], weight_ref[j, at, core]), (beside_ref[j], other_ref[j, at])):
                part = dot(rows, block, LAST)
                acc = part if acc is None else acc + part
        out_ref[step] = acc.astype(out_ref.dtype)


def project(summed, beside, by_core, other):
    return pl.pallas_call(
        project_kernel,
        in_specs=[VMEM] * 4,
        out_specs=VMEM,
        out_shape=jax.ShapeDtypeStruct((4, summed.shape[1], by_core.shape[3]), jnp.bfloat16),
        compiler_params=pltpu.CompilerParams(vmem_limit_bytes=24 * 2**20),
    )(summed, beside, by_core, other)


def ring(size, step, stride):
    block = size // stride * stride
    return [(i, (i // stride + step) * stride % block + i % stride) for i in range(size)]


def swap(size):
    return [(i, i ^ 1) for i in range(size)]


def z_hop(x, step):
    return lax.ppermute(x, "group", ring(2 * SPLIT, step, 2))


def x_swap(x):
    return lax.ppermute(x, "group", swap(2 * SPLIT))


def after(value, *done):
    return lax.optimization_barrier((value, *done))[0]


def add_low(a, b):
    return (a.astype(jnp.float32) + b.astype(jnp.float32)).astype(jnp.bfloat16)


def on_device(queries, response_kv, grad_out, prefix_kv, kv_weight, resp_len, prefix_len, owner):
    group = lax.axis_index("group")
    z, x = group // 2, group % 2
    dh = prefix_kv.shape[3]
    scale = dh ** (-0.5)
    scale2 = scale * LOG2E
    q, g, own, prefix = queries[0], grad_out[0], response_kv[0], prefix_kv[0]
    lens = (prefix_len, resp_len)
    by_core = kv_weight.reshape(2, 4, 2, kv_weight.shape[1] // 8, dh)

    keys = prefix.shape[1] // SPLIT
    half_way = SPLIT // 2
    owner_z = owner[0] // 2
    away = lax.rem(z - owner_z + SPLIT, SPLIT)

    def branch(holder):
        def body(by_core, q, g, own, *pieces):
            got = {}
            for step in (4, 3, 5, 2, 6, 1, 7):
                pairs = [(2 * at + c, 2 * ((at + step) % SPLIT) + c) for at in (holder, holder + half_way) for c in (0, 1)]
                got[step] = lax.ppermute(pieces[step], "group", pairs)
            by_core, q, got[4] = lax.optimization_barrier((by_core, q, got[4]))
            other = lax.ppermute(lend(by_core), "tensor", swap(8))
            stats = forward(lens, q, g, (None,), [own], None, scale2, False)
            held = pieces[0]
            for step in range(1, SPLIT):
                held = jnp.where(away == step, got[step], held)
            return held, stats, other

        return body

    held, stats, other = lax.switch(
        lax.rem(owner_z, half_way), [branch(k) for k in range(half_way)], by_core, q, g, own, *cut(prefix, keys)
    )
    held = jnp.where(x == owner[0] % 2, held, x_swap(held))

    pieces = {0: held}
    new = [0]
    up = down = held
    for hop in range(1, half_way + 1):
        up = z_hop(up, 1)
        if hop < half_way:
            down = z_hop(down, -1)
        stats = forward(lens, q, g, tuple(new), [pieces[k] for k in new], stats, scale2, False)
        new = [SPLIT - hop]
        if hop < half_way:
            up, down, stats = lax.optimization_barrier((up, down, stats))
            pieces[hop] = down
            new.append(hop)
        else:
            up, stats = lax.optimization_barrier((up, stats))
        pieces[SPLIT - hop] = up
    stats = forward(lens, q, g, tuple(new), [pieces[k] for k in new], stats, scale2, True)

    dq, (grad,) = backward(lens, q, g, stats, (half_way,), [pieces[half_way]], None, scale, scale2, False)
    up, down = z_hop(grad, 1), None
    for left in range(half_way - 1, 0, -1):
        new = (left, SPLIT - left)
        dq, grads = backward(lens, q, g, stats, new, [pieces[k] for k in new], dq, scale, scale2, False)
        up, dq, *grads = lax.optimization_barrier((up, dq, *grads))
        up = z_hop(add_low(grads[0], up), 1)
        down = z_hop(grads[1] if down is None else add_low(grads[1], down), -1)
    dq, (grad,) = backward(lens, q, g, stats, (0,), [pieces[0]], dq, scale, scale2, False)
    up, down, dq, grad = lax.optimization_barrier((up, down, dq, grad))
    half = keys // 2

    def rows_of(at):
        up_, down_, grad_ = (lax.dynamic_slice_in_dim(v, at * half, half, 1).astype(jnp.float32) for v in (up, down, grad))
        return up_ + down_ + grad_

    swapped = x_swap(rows_of(1 - x).astype(jnp.bfloat16))
    dq, (own_grad,) = backward(lens, q, g, stats, (None,), [own], dq, scale, scale2, True)
    swapped, dq, own_grad = lax.optimization_barrier((swapped, dq, own_grad))
    summed = (rows_of(x) + swapped.astype(jnp.float32)).astype(jnp.bfloat16)

    beside = lax.ppermute(summed, "tensor", swap(8))
    shares = project(summed, beside, by_core, other)
    result = shares[0].astype(jnp.float32)
    for k in (1, 2, 3):
        result = result + lax.ppermute(shares[k], "tensor", ring(8, k, 2)).astype(jnp.float32)
    return dq[None], own_grad[None], result.astype(jnp.bfloat16)


def solution(mesh):
    in_specs = (
        P(("prompt", "group"), None, "tensor"),
        P(("prompt", "group"), None, None, "tensor"),
        P(("prompt", "group"), None, "tensor"),
        P(("prompt", "group"), None, None, "tensor"),
        P(None, None, "tensor"),
        P(("prompt", "group")),
        P("prompt"),
        P("prompt"),
    )
    out_specs = (
        P(("prompt", "group"), None, "tensor"),
        P(("prompt", "group"), None, None, "tensor"),
        P(("prompt", "group"), "tensor"),
    )
    return jax.shard_map(
        on_device, mesh=mesh, in_specs=in_specs, out_specs=out_specs, check_vma=False
    )
```

```python
import functools

import jax
import jax.numpy as jnp
from jax import lax
from jax.experimental import pallas as pl
from jax.experimental.pallas import tpu as pltpu
from jax.sharding import PartitionSpec as P

LAST = (((1,), (1,)), ((), ()))
PLAIN = (((1,), (0,)), ((), ()))
LOG2E = 1.4426950408889634
SPLIT = 8
SMEM = pl.BlockSpec(memory_space=pltpu.SMEM)
VMEM = pl.BlockSpec(memory_space=pltpu.VMEM)
ANY = pl.BlockSpec(memory_space=pl.ANY)


def dot(a, b, dims=PLAIN):
    return lax.dot_general(a, b, dims, preferred_element_type=jnp.float32)


def block_scores(kind, keys, q, live_ref, scale2):
    s = dot(keys, q, LAST) * scale2
    at = lax.broadcasted_iota(jnp.int32, s.shape, 0)
    if kind is None:
        ok = at <= lax.broadcasted_iota(jnp.int32, s.shape, 1)
    else:
        base = lax.rem(lax.axis_index("group") // 2 + kind, SPLIT) * s.shape[0]
        ok = at < live_ref[0] - base
    return jnp.where(ok, s, -jnp.inf)


def forward_kernel(kinds, scale2, first, last, heads, live_ref, rows_ref, q_ref, g_ref, *refs):
    n = len(kinds)
    kv = refs[:n]
    out_ref = refs[-1]
    dh = q_ref.shape[1] // heads

    @pl.loop(0, heads)
    def _(h):
        cols = pl.ds(pl.multiple_of(h * dh, dh), dh)
        q = q_ref[:, cols]
        g = g_ref[:, cols]
        if first:
            m = l = r = None
        else:
            m, l, r = refs[n][h, 0:1], refs[n][h, 1:2], refs[n][h, 2:3]
        for kind, ref in zip(kinds, kv):
            s = block_scores(kind, ref[0], q, live_ref, scale2)
            top = jnp.max(s, 0, keepdims=True)
            new = top if m is None else jnp.maximum(m, top)
            p = jnp.exp2(s - new)
            dp = dot(ref[1], g, LAST)
            lb = jnp.sum(p, 0, keepdims=True)
            rb = jnp.sum(p * dp, 0, keepdims=True)
            if m is None:
                l, r = lb, rb
            else:
                a = jnp.exp2(m - new)
                l, r = l * a + lb, r * a + rb
            m = new
        if last:
            live = lax.broadcasted_iota(jnp.int32, m.shape, 1) < rows_ref[0]
            m = jnp.where(live, m + jnp.log2(l), jnp.inf)
            r = r / l
        out_ref[h, 0:1] = m
        out_ref[h, 1:2] = l
        out_ref[h, 2:3] = r


def forward(lens, q, g, kinds, blocks, stats, scale2, last):
    rows, width = q.shape
    dh = blocks[0].shape[2]
    heads = width // dh
    first = stats is None
    keys = sum(b.shape[1] for b in blocks)
    n = 2 + len(blocks) + (not first)
    return pl.pallas_call(
        functools.partial(forward_kernel, kinds, scale2, first, last, heads),
        in_specs=[SMEM] * 2 + [VMEM] * n,
        out_specs=VMEM,
        out_shape=jax.ShapeDtypeStruct((heads, 8, rows), jnp.float32),
        cost_estimate=pl.CostEstimate(flops=4 * heads * rows * keys * dh, bytes_accessed=4 * q.size, transcendentals=heads * rows * keys),
        compiler_params=pltpu.CompilerParams(vmem_limit_bytes=24 * 2**20),
    )(*lens, q, g, *blocks, *([] if first else [stats]))


def backward_kernel(kinds, scale, scale2, first, last, heads, live_ref, rows_ref, q_ref, g_ref, stat_ref, *refs):
    n = len(kinds)
    kv, refs = refs[:n], refs[n:]
    if not first:
        dq_in, refs = refs[0], refs[1:]
    dq_ref, outs, accs = refs[0], refs[1:1 + n], refs[1 + n:]
    dh = q_ref.shape[1] // heads
    for acc in accs:
        acc[...] = jnp.zeros_like(acc)

    @pl.loop(0, heads)
    def _(h):
        cols = pl.ds(pl.multiple_of(h * dh, dh), dh)
        q = q_ref[:, cols]
        g = g_ref[:, cols]
        mm = stat_ref[h, 0:1]
        rr = stat_ref[h, 2:3]
        dqt = None if first else dq_in[cols, :]
        for kind, ref, acc in zip(kinds, kv, accs):
            keys = ref[0]
            s = block_scores(kind, keys, q, live_ref, scale2)
            p = jnp.exp2(s - mm)
            dp = dot(ref[1], g, LAST)
            ds = (p * (dp - rr)).astype(jnp.bfloat16)
            acc[1] += dot(p.astype(jnp.bfloat16), g)
            acc[0] += dot(ds, q)
            part = dot(keys.T, ds)
            dqt = part if dqt is None else dqt + part
        if last:
            dq_ref[:, cols] = (dqt.T * scale).astype(dq_ref.dtype)
        else:
            dq_ref[cols, :] = dqt

    for out, acc in zip(outs, accs):
        out[0] = (acc[0] * scale).astype(out.dtype)
        out[1] = acc[1].astype(out.dtype)


def backward(lens, q, g, stats, kinds, blocks, dq, scale, scale2, last):
    rows, width = q.shape
    dh = blocks[0].shape[2]
    heads = width // dh
    first = dq is None
    keys = sum(b.shape[1] for b in blocks)
    if last:
        dq_shape = jax.ShapeDtypeStruct((rows, width), jnp.bfloat16)
    else:
        dq_shape = jax.ShapeDtypeStruct((width, rows), jnp.float32)
    n = 3 + len(blocks) + (not first)
    res = pl.pallas_call(
        functools.partial(backward_kernel, kinds, scale, scale2, first, last, heads),
        in_specs=[SMEM] * 2 + [VMEM] * n,
        out_specs=[VMEM] * (1 + len(blocks)),
        out_shape=[dq_shape] + [jax.ShapeDtypeStruct(b.shape, jnp.bfloat16) for b in blocks],
        scratch_shapes=[pltpu.VMEM(b.shape, jnp.float32) for b in blocks],
        cost_estimate=pl.CostEstimate(flops=10 * heads * rows * keys * dh, bytes_accessed=4 * q.size, transcendentals=heads * rows * keys),
        compiler_params=pltpu.CompilerParams(vmem_limit_bytes=24 * 2**20),
    )(*lens, q, g, stats, *blocks, *([] if first else [dq]))
    return res[0], list(res[1:])


def cut_kernel(keys, prefix_ref, weight_ref, *refs):
    outs, lent_ref, sems = refs[:SPLIT], refs[SPLIT], refs[SPLIT + 1]
    z = lax.axis_index("group") // 2
    core = lax.rem(lax.axis_index("tensor"), 2)
    copies = []
    for step in (4, 3, 5, 2, 6, 1, 7, 0):
        at = pl.multiple_of(lax.rem(z + step, SPLIT) * keys, keys)
        copies.append(pltpu.make_async_copy(prefix_ref.at[:, pl.ds(at, keys), :], outs[step], sems.at[step]))
    copies.append(pltpu.make_async_copy(weight_ref.at[:, :, 1 - core], lent_ref, sems.at[SPLIT]))
    for copy in copies:
        copy.start()
    for copy in copies:
        copy.wait()


def cut(prefix, by_core, keys):
    shape = (prefix.shape[0], keys, prefix.shape[2])
    lent = by_core.shape[:2] + by_core.shape[3:]
    res = pl.pallas_call(
        functools.partial(cut_kernel, keys),
        in_specs=[ANY] * 2,
        out_specs=[ANY] * SPLIT + [VMEM],
        out_shape=[jax.ShapeDtypeStruct(shape, prefix.dtype)] * SPLIT + [jax.ShapeDtypeStruct(lent, by_core.dtype)],
        scratch_shapes=[pltpu.SemaphoreType.DMA((SPLIT + 1,))],
    )(prefix, by_core)
    return res[:SPLIT], res[SPLIT]


def project_kernel(summed_ref, beside_ref, weight_ref, other_ref, out_ref, held_ref, sems):
    tensor = lax.axis_index("tensor")
    y, core = tensor // 2, lax.rem(tensor, 2)
    copies = []
    for step in range(4):
        at = lax.rem(y + step, 4)
        mine = pltpu.make_async_copy(weight_ref.at[:, at, core], held_ref.at[step, 0], sems.at[step, 0])
        theirs = pltpu.make_async_copy(other_ref.at[:, at], held_ref.at[step, 1], sems.at[step, 1])
        mine.start()
        theirs.start()
        copies.append((mine, theirs))
    for step in range(4):
        acc = None
        for c, rows in enumerate((summed_ref, beside_ref)):
            copies[step][c].wait()
            for j in range(2):
                part = dot(rows[j], held_ref[step, c, j], LAST)
                acc = part if acc is None else acc + part
        out_ref[step] = acc.astype(out_ref.dtype)


def project(summed, beside, by_core, other):
    cols, dh = by_core.shape[3:]
    return pl.pallas_call(
        project_kernel,
        in_specs=[VMEM] * 2 + [ANY] * 2,
        out_specs=VMEM,
        out_shape=jax.ShapeDtypeStruct((4, summed.shape[1], cols), jnp.bfloat16),
        scratch_shapes=[pltpu.VMEM((4, 2, 2, cols, dh), by_core.dtype), pltpu.SemaphoreType.DMA((4, 2))],
        compiler_params=pltpu.CompilerParams(vmem_limit_bytes=24 * 2**20),
    )(summed, beside, by_core, other)


def ring(size, step, stride):
    block = size // stride * stride
    return [(i, (i // stride + step) * stride % block + i % stride) for i in range(size)]


def swap(size):
    return [(i, i ^ 1) for i in range(size)]


def z_hop(x, step):
    return lax.ppermute(x, "group", ring(2 * SPLIT, step, 2))


def x_swap(x):
    return lax.ppermute(x, "group", swap(2 * SPLIT))


def add_low(a, b):
    return (a.astype(jnp.float32) + b.astype(jnp.float32)).astype(jnp.bfloat16)


def on_device(queries, response_kv, grad_out, prefix_kv, kv_weight, resp_len, prefix_len, owner):
    group = lax.axis_index("group")
    z, x = group // 2, group % 2
    dh = prefix_kv.shape[3]
    scale = dh ** (-0.5)
    scale2 = scale * LOG2E
    q, g, own, prefix = queries[0], grad_out[0], response_kv[0], prefix_kv[0]
    lens = (prefix_len, resp_len)
    by_core = kv_weight.reshape(2, 4, 2, kv_weight.shape[1] // 8, dh)

    keys = prefix.shape[1] // SPLIT
    half_way = SPLIT // 2
    owner_z = owner[0] // 2
    away = lax.rem(z - owner_z + SPLIT, SPLIT)

    def branch(holder):
        def body(*pieces):
            got = {}
            for step in (4, 3, 5, 2, 6, 1, 7):
                pairs = [(2 * at + c, 2 * ((at + step) % SPLIT) + c) for at in (holder, holder + half_way) for c in (0, 1)]
                got[step] = lax.ppermute(pieces[step], "group", pairs)
            held = pieces[0]
            for step in range(1, SPLIT):
                held = jnp.where(away == step, got[step], held)
            return held

        return body

    pieces, lent = cut(prefix, by_core, keys)
    held = lax.switch(lax.rem(owner_z, half_way), [branch(k) for k in range(half_way)], *pieces)
    held = jnp.where(x == owner[0] % 2, held, x_swap(held))

    pieces = {0: held}
    new = [0]
    up = down = held
    stats = None
    other = lax.ppermute(lent, "tensor", swap(8))
    for hop in range(1, half_way + 1):
        up = z_hop(up, 1)
        if hop < half_way:
            down = z_hop(down, -1)
        if hop == 1:
            stats = forward(lens, q, g, (None, 0), [own, held], None, scale2, False)
        else:
            stats = forward(lens, q, g, tuple(new), [pieces[k] for k in new], stats, scale2, False)
        new = [SPLIT - hop]
        if hop < half_way:
            up, down, stats, other = lax.optimization_barrier((up, down, stats, other))
            pieces[hop] = down
            new.append(hop)
        else:
            up, stats = lax.optimization_barrier((up, stats))
        pieces[SPLIT - hop] = up
    stats = forward(lens, q, g, tuple(new), [pieces[k] for k in new], stats, scale2, True)

    dq, (grad,) = backward(lens, q, g, stats, (half_way,), [pieces[half_way]], None, scale, scale2, False)
    up, down = z_hop(grad, 1), None
    for left in range(half_way - 1, 0, -1):
        new = (left, SPLIT - left)
        dq, grads = backward(lens, q, g, stats, new, [pieces[k] for k in new], dq, scale, scale2, False)
        up, dq, *grads = lax.optimization_barrier((up, dq, *grads))
        up = z_hop(add_low(grads[0], up), 1)
        down = z_hop(grads[1] if down is None else add_low(grads[1], down), -1)
    dq, (grad,) = backward(lens, q, g, stats, (0,), [pieces[0]], dq, scale, scale2, False)
    up, down, dq, grad = lax.optimization_barrier((up, down, dq, grad))
    half = keys // 2

    def rows_of(at):
        up_, down_, grad_ = (lax.dynamic_slice_in_dim(v, at * half, half, 1).astype(jnp.float32) for v in (up, down, grad))
        return up_ + down_ + grad_

    swapped = x_swap(rows_of(1 - x).astype(jnp.bfloat16))
    dq, (own_grad,) = backward(lens, q, g, stats, (None,), [own], dq, scale, scale2, True)
    swapped, dq, own_grad = lax.optimization_barrier((swapped, dq, own_grad))
    summed = (rows_of(x) + swapped.astype(jnp.float32)).astype(jnp.bfloat16)

    beside = lax.ppermute(summed, "tensor", swap(8))
    shares = project(summed, beside, by_core, other)
    result = shares[0].astype(jnp.float32)
    for k in (1, 2, 3):
        result = result + lax.ppermute(shares[k], "tensor", ring(8, k, 2)).astype(jnp.float32)
    return dq[None], own_grad[None], result.astype(jnp.bfloat16)


def solution(mesh):
    in_specs = (
        P(("prompt", "group"), None, "tensor"),
        P(("prompt", "group"), None, None, "tensor"),
        P(("prompt", "group"), None, "tensor"),
        P(("prompt", "group"), None, None, "tensor"),
        P(None, None, "tensor"),
        P(("prompt", "group")),
        P("prompt"),
        P("prompt"),
    )
    out_specs = (
        P(("prompt", "group"), None, "tensor"),
        P(("prompt", "group"), None, None, "tensor"),
        P(("prompt", "group"), "tensor"),
    )
    return jax.shard_map(
        on_device, mesh=mesh, in_specs=in_specs, out_specs=out_specs, check_vma=False
    )
```

```python
import functools

import jax
import jax.numpy as jnp
from jax import lax
from jax.experimental import pallas as pl
from jax.experimental.pallas import tpu as pltpu
from jax.sharding import PartitionSpec as P

LAST = (((1,), (1,)), ((), ()))
PLAIN = (((1,), (0,)), ((), ()))
LOG2E = 1.4426950408889634
SPLIT = 8
SMEM = pl.BlockSpec(memory_space=pltpu.SMEM)
VMEM = pl.BlockSpec(memory_space=pltpu.VMEM)
ANY = pl.BlockSpec(memory_space=pl.ANY)


def dot(a, b, dims=PLAIN):
    return lax.dot_general(a, b, dims, preferred_element_type=jnp.float32)


def block_scores(kind, keys, q, live_ref, scale2):
    s = dot(keys, q, LAST) * scale2
    at = lax.broadcasted_iota(jnp.int32, s.shape, 0)
    if kind is None:
        ok = at <= lax.broadcasted_iota(jnp.int32, s.shape, 1)
    else:
        base = lax.rem(lax.axis_index("group") // 2 + kind, SPLIT) * s.shape[0]
        ok = at < live_ref[0] - base
    return jnp.where(ok, s, -jnp.inf)


def forward_kernel(kinds, scale2, first, last, heads, live_ref, rows_ref, q_ref, g_ref, *refs):
    n = len(kinds)
    kv = refs[:n]
    out_ref = refs[-1]
    dh = q_ref.shape[1] // heads

    @pl.loop(0, heads, unroll=2)
    def _(h):
        cols = pl.ds(pl.multiple_of(h * dh, dh), dh)
        q = q_ref[:, cols]
        g = g_ref[:, cols]
        if first:
            m = l = r = None
        else:
            m, l, r = refs[n][h, 0:1], refs[n][h, 1:2], refs[n][h, 2:3]
        for kind, ref in zip(kinds, kv):
            s = block_scores(kind, ref[0], q, live_ref, scale2)
            top = jnp.max(s, 0, keepdims=True)
            new = top if m is None else jnp.maximum(m, top)
            p = jnp.exp2(s - new)
            dp = dot(ref[1], g, LAST)
            lb = jnp.sum(p, 0, keepdims=True)
            rb = jnp.sum(p * dp, 0, keepdims=True)
            if m is None:
                l, r = lb, rb
            else:
                a = jnp.exp2(m - new)
                l, r = l * a + lb, r * a + rb
            m = new
        if last:
            live = lax.broadcasted_iota(jnp.int32, m.shape, 1) < rows_ref[0]
            m = jnp.where(live, m + jnp.log2(l), jnp.inf)
            r = r / l
        out_ref[h, 0:1] = m
        out_ref[h, 1:2] = l
        out_ref[h, 2:3] = r


def forward(lens, q, g, kinds, blocks, stats, scale2, last):
    rows, width = q.shape
    dh = blocks[0].shape[2]
    heads = width // dh
    first = stats is None
    keys = sum(b.shape[1] for b in blocks)
    n = 2 + len(blocks) + (not first)
    return pl.pallas_call(
        functools.partial(forward_kernel, kinds, scale2, first, last, heads),
        in_specs=[SMEM] * 2 + [VMEM] * n,
        out_specs=VMEM,
        out_shape=jax.ShapeDtypeStruct((heads, 8, rows), jnp.float32),
        cost_estimate=pl.CostEstimate(flops=4 * heads * rows * keys * dh, bytes_accessed=4 * q.size, transcendentals=heads * rows * keys),
        compiler_params=pltpu.CompilerParams(vmem_limit_bytes=16 * 2**20),
    )(*lens, q, g, *blocks, *([] if first else [stats]))


def backward_kernel(kinds, scale, scale2, first, last, heads, live_ref, rows_ref, q_ref, g_ref, stat_ref, *refs):
    n = len(kinds)
    kv, refs = refs[:n], refs[n:]
    if not first:
        dq_in, refs = refs[0], refs[1:]
    dq_ref, outs, accs = refs[0], refs[1:1 + n], refs[1 + n:]
    dh = q_ref.shape[1] // heads
    for acc in accs:
        acc[...] = jnp.zeros_like(acc)

    @pl.loop(0, heads, unroll=2)
    def _(h):
        cols = pl.ds(pl.multiple_of(h * dh, dh), dh)
        q = q_ref[:, cols]
        g = g_ref[:, cols]
        mm = stat_ref[h, 0:1]
        rr = stat_ref[h, 2:3]
        dqt = None if first else dq_in[cols, :]
        for kind, ref, acc in zip(kinds, kv, accs):
            keys = ref[0]
            s = block_scores(kind, keys, q, live_ref, scale2)
            p = jnp.exp2(s - mm)
            dp = dot(ref[1], g, LAST)
            ds = (p * (dp - rr)).astype(jnp.bfloat16)
            acc[1] += dot(p.astype(jnp.bfloat16), g)
            acc[0] += dot(ds, q)
            part = dot(keys.T, ds)
            dqt = part if dqt is None else dqt + part
        if last:
            dq_ref[:, cols] = (dqt.T * scale).astype(dq_ref.dtype)
        else:
            dq_ref[cols, :] = dqt

    for out, acc in zip(outs, accs):
        out[0] = (acc[0] * scale).astype(out.dtype)
        out[1] = acc[1].astype(out.dtype)


def backward(lens, q, g, stats, kinds, blocks, dq, scale, scale2, last):
    rows, width = q.shape
    dh = blocks[0].shape[2]
    heads = width // dh
    first = dq is None
    keys = sum(b.shape[1] for b in blocks)
    if last:
        dq_shape = jax.ShapeDtypeStruct((rows, width), jnp.bfloat16)
    else:
        dq_shape = jax.ShapeDtypeStruct((width, rows), jnp.float32)
    n = 3 + len(blocks) + (not first)
    res = pl.pallas_call(
        functools.partial(backward_kernel, kinds, scale, scale2, first, last, heads),
        in_specs=[SMEM] * 2 + [VMEM] * n,
        out_specs=[VMEM] * (1 + len(blocks)),
        out_shape=[dq_shape] + [jax.ShapeDtypeStruct(b.shape, jnp.bfloat16) for b in blocks],
        scratch_shapes=[pltpu.VMEM(b.shape, jnp.float32) for b in blocks],
        cost_estimate=pl.CostEstimate(flops=10 * heads * rows * keys * dh, bytes_accessed=4 * q.size, transcendentals=heads * rows * keys),
        compiler_params=pltpu.CompilerParams(vmem_limit_bytes=16 * 2**20),
    )(*lens, q, g, stats, *blocks, *([] if first else [dq]))
    return res[0], list(res[1:])


def cut_kernel(keys, prefix_ref, *refs):
    outs, sems = refs[:SPLIT], refs[SPLIT]
    z = lax.axis_index("group") // 2
    copies = []
    for step in (4, 3, 5, 2, 6, 1, 7, 0):
        at = pl.multiple_of(lax.rem(z + step, SPLIT) * keys, keys)
        copies.append(pltpu.make_async_copy(prefix_ref.at[:, pl.ds(at, keys), :], outs[step], sems.at[step]))
    for copy in copies:
        copy.start()
    for copy in copies:
        copy.wait()


def cut(prefix, keys):
    shape = (prefix.shape[0], keys, prefix.shape[2])
    return pl.pallas_call(
        functools.partial(cut_kernel, keys),
        in_specs=[ANY],
        out_specs=[ANY] * SPLIT,
        out_shape=[jax.ShapeDtypeStruct(shape, prefix.dtype)] * SPLIT,
        scratch_shapes=[pltpu.SemaphoreType.DMA((SPLIT,))],
    )(prefix)


def lend_kernel(weight_ref, out_ref, sems):
    core = lax.rem(lax.axis_index("tensor"), 2)
    copies = []
    for at in range(4):
        copies.append(pltpu.make_async_copy(weight_ref.at[:, at, 1 - core], out_ref.at[:, at], sems.at[at]))
        copies[-1].start()
    for copy in copies:
        copy.wait()


def lend(by_core):
    shape = by_core.shape[:2] + by_core.shape[3:]
    return pl.pallas_call(
        lend_kernel,
        in_specs=[ANY],
        out_specs=VMEM,
        out_shape=jax.ShapeDtypeStruct(shape, by_core.dtype),
        scratch_shapes=[pltpu.SemaphoreType.DMA((4,))],
    )(by_core)


def project_kernel(summed_ref, beside_ref, weight_ref, other_ref, out_ref, held_ref, sems):
    tensor = lax.axis_index("tensor")
    y, core = tensor // 2, lax.rem(tensor, 2)
    copies = []
    for step in range(4):
        at = lax.rem(y + step, 4)
        mine = pltpu.make_async_copy(weight_ref.at[:, at, core], held_ref.at[step, 0], sems.at[step, 0])
        theirs = pltpu.make_async_copy(other_ref.at[:, at], held_ref.at[step, 1], sems.at[step, 1])
        mine.start()
        theirs.start()
        copies.append((mine, theirs))
    for step in range(4):
        acc = None
        for c, rows in enumerate((summed_ref, beside_ref)):
            copies[step][c].wait()
            for j in range(2):
                part = dot(rows[j], held_ref[step, c, j], LAST)
                acc = part if acc is None else acc + part
        out_ref[step] = acc.astype(out_ref.dtype)


def project(summed, beside, by_core, other):
    cols, dh = by_core.shape[3:]
    return pl.pallas_call(
        project_kernel,
        in_specs=[VMEM] * 2 + [ANY] * 2,
        out_specs=VMEM,
        out_shape=jax.ShapeDtypeStruct((4, summed.shape[1], cols), jnp.bfloat16),
        scratch_shapes=[pltpu.VMEM((4, 2, 2, cols, dh), by_core.dtype), pltpu.SemaphoreType.DMA((4, 2))],
        compiler_params=pltpu.CompilerParams(vmem_limit_bytes=16 * 2**20),
    )(summed, beside, by_core, other)


def ring(size, step, stride):
    block = size // stride * stride
    return [(i, (i // stride + step) * stride % block + i % stride) for i in range(size)]


def swap(size):
    return [(i, i ^ 1) for i in range(size)]


def z_hop(x, step):
    return lax.ppermute(x, "group", ring(2 * SPLIT, step, 2))


def x_swap(x):
    return lax.ppermute(x, "group", swap(2 * SPLIT))


def add_low(a, b):
    return (a.astype(jnp.float32) + b.astype(jnp.float32)).astype(jnp.bfloat16)


def on_device(queries, response_kv, grad_out, prefix_kv, kv_weight, resp_len, prefix_len, owner):
    group = lax.axis_index("group")
    z, x = group // 2, group % 2
    dh = prefix_kv.shape[3]
    scale = dh ** (-0.5)
    scale2 = scale * LOG2E
    q, g, own, prefix = queries[0], grad_out[0], response_kv[0], prefix_kv[0]
    lens = (prefix_len, resp_len)
    by_core = kv_weight.reshape(2, 4, 2, kv_weight.shape[1] // 8, dh)

    keys = prefix.shape[1] // SPLIT
    half_way = SPLIT // 2
    owner_z = owner[0] // 2
    away = lax.rem(z - owner_z + SPLIT, SPLIT)

    def branch(holder):
        def body(*pieces):
            got = {}
            for step in (4, 3, 5, 2, 6, 1, 7):
                pairs = [(2 * at + c, 2 * ((at + step) % SPLIT) + c) for at in (holder, holder + half_way) for c in (0, 1)]
                got[step] = lax.ppermute(pieces[step], "group", pairs)
            held = pieces[0]
            for step in range(1, SPLIT):
                held = jnp.where(away == step, got[step], held)
            return held

        return body

    held = lax.switch(lax.rem(owner_z, half_way), [branch(k) for k in range(half_way)], *cut(prefix, keys))
    held, by_core = lax.optimization_barrier((held, by_core))
    swapped, lent = lax.optimization_barrier((x_swap(held), lend(by_core)))
    held = jnp.where(x == owner[0] % 2, held, swapped)

    pieces = {0: held}
    new = [0]
    up = down = held
    stats = None
    other = lax.ppermute(lent, "tensor", swap(8))
    for hop in range(1, half_way + 1):
        up = z_hop(up, 1)
        if hop < half_way:
            down = z_hop(down, -1)
        if hop == 1:
            stats = forward(lens, q, g, (None, 0), [own, held], None, scale2, False)
        else:
            stats = forward(lens, q, g, tuple(new), [pieces[k] for k in new], stats, scale2, False)
        new = [SPLIT - hop]
        if hop < half_way:
            up, down, stats, other = lax.optimization_barrier((up, down, stats, other))
            pieces[hop] = down
            new.append(hop)
        else:
            up, stats = lax.optimization_barrier((up, stats))
        pieces[SPLIT - hop] = up
    stats = forward(lens, q, g, tuple(new), [pieces[k] for k in new], stats, scale2, True)

    dq, (grad,) = backward(lens, q, g, stats, (half_way,), [pieces[half_way]], None, scale, scale2, False)
    up, down = z_hop(grad, 1), None
    for left in range(half_way - 1, 0, -1):
        new = (left, SPLIT - left)
        dq, grads = backward(lens, q, g, stats, new, [pieces[k] for k in new], dq, scale, scale2, False)
        up, dq, *grads = lax.optimization_barrier((up, dq, *grads))
        up = z_hop(add_low(grads[0], up), 1)
        down = z_hop(grads[1] if down is None else add_low(grads[1], down), -1)
    dq, (grad,) = backward(lens, q, g, stats, (0,), [pieces[0]], dq, scale, scale2, False)
    up, down, dq, grad = lax.optimization_barrier((up, down, dq, grad))
    half = keys // 2

    def rows_of(at):
        up_, down_, grad_ = (lax.dynamic_slice_in_dim(v, at * half, half, 1).astype(jnp.float32) for v in (up, down, grad))
        return up_ + down_ + grad_

    swapped = x_swap(rows_of(1 - x).astype(jnp.bfloat16))
    dq, (own_grad,) = backward(lens, q, g, stats, (None,), [own], dq, scale, scale2, True)
    swapped, dq, own_grad = lax.optimization_barrier((swapped, dq, own_grad))
    summed = (rows_of(x) + swapped.astype(jnp.float32)).astype(jnp.bfloat16)

    beside = lax.ppermute(summed, "tensor", swap(8))
    shares = project(summed, beside, by_core, other)
    result = shares[0].astype(jnp.float32)
    for k in (1, 2, 3):
        result = result + lax.ppermute(shares[k], "tensor", ring(8, k, 2)).astype(jnp.float32)
    return dq[None], own_grad[None], result.astype(jnp.bfloat16)


def solution(mesh):
    in_specs = (
        P(("prompt", "group"), None, "tensor"),
        P(("prompt", "group"), None, None, "tensor"),
        P(("prompt", "group"), None, "tensor"),
        P(("prompt", "group"), None, None, "tensor"),
        P(None, None, "tensor"),
        P(("prompt", "group")),
        P("prompt"),
        P("prompt"),
    )
    out_specs = (
        P(("prompt", "group"), None, "tensor"),
        P(("prompt", "group"), None, None, "tensor"),
        P(("prompt", "group"), "tensor"),
    )
    return jax.shard_map(
        on_device, mesh=mesh, in_specs=in_specs, out_specs=out_specs, check_vma=False
    )
```

```python
import functools

import jax
import jax.numpy as jnp
from jax import lax
from jax.experimental import pallas as pl
from jax.experimental.pallas import tpu as pltpu
from jax.sharding import PartitionSpec as P

LAST = (((1,), (1,)), ((), ()))
PLAIN = (((1,), (0,)), ((), ()))
LOG2E = 1.4426950408889634
SPLIT = 8
SMEM = pl.BlockSpec(memory_space=pltpu.SMEM)
VMEM = pl.BlockSpec(memory_space=pltpu.VMEM)
ANY = pl.BlockSpec(memory_space=pl.ANY)


def dot(a, b, dims=PLAIN):
    return lax.dot_general(a, b, dims, preferred_element_type=jnp.float32)


def block_scores(kind, keys, q, live_ref, scale2):
    s = dot(keys, q, LAST) * scale2
    at = lax.broadcasted_iota(jnp.int32, s.shape, 0)
    if kind is None:
        ok = at <= lax.broadcasted_iota(jnp.int32, s.shape, 1)
    else:
        base = lax.rem(lax.axis_index("group") // 2 + kind, SPLIT) * s.shape[0]
        ok = at < live_ref[0] - base
    return jnp.where(ok, s, -jnp.inf)


def forward_kernel(kinds, scale2, first, last, heads, live_ref, rows_ref, q_ref, g_ref, *refs):
    n = len(kinds)
    kv = refs[:n]
    out_ref = refs[-1]
    dh = q_ref.shape[1] // heads

    @pl.loop(0, heads, unroll=2)
    def _(h):
        cols = pl.ds(pl.multiple_of(h * dh, dh), dh)
        q = q_ref[:, cols]
        g = g_ref[:, cols]
        if first:
            m = l = r = None
        else:
            m, l, r = refs[n][h, 0:1], refs[n][h, 1:2], refs[n][h, 2:3]
        for kind, ref in zip(kinds, kv):
            s = block_scores(kind, ref[0], q, live_ref, scale2)
            top = jnp.max(s, 0, keepdims=True)
            new = top if m is None else jnp.maximum(m, top)
            p = jnp.exp2(s - new)
            dp = dot(ref[1], g, LAST)
            lb = jnp.sum(p, 0, keepdims=True)
            rb = jnp.sum(p * dp, 0, keepdims=True)
            if m is None:
                l, r = lb, rb
            else:
                a = jnp.exp2(m - new)
                l, r = l * a + lb, r * a + rb
            m = new
        if last:
            live = lax.broadcasted_iota(jnp.int32, m.shape, 1) < rows_ref[0]
            m = jnp.where(live, m + jnp.log2(l), jnp.inf)
            r = r / l
        out_ref[h, 0:1] = m
        out_ref[h, 1:2] = l
        out_ref[h, 2:3] = r


def forward(lens, q, g, kinds, blocks, stats, scale2, last):
    rows, width = q.shape
    dh = blocks[0].shape[2]
    heads = width // dh
    first = stats is None
    keys = sum(b.shape[1] for b in blocks)
    n = 2 + len(blocks) + (not first)
    return pl.pallas_call(
        functools.partial(forward_kernel, kinds, scale2, first, last, heads),
        in_specs=[SMEM] * 2 + [VMEM] * n,
        out_specs=VMEM,
        out_shape=jax.ShapeDtypeStruct((heads, 8, rows), jnp.float32),
        cost_estimate=pl.CostEstimate(flops=4 * heads * rows * keys * dh, bytes_accessed=4 * q.size, transcendentals=heads * rows * keys),
        compiler_params=pltpu.CompilerParams(vmem_limit_bytes=16 * 2**20),
    )(*lens, q, g, *blocks, *([] if first else [stats]))


def backward_kernel(kinds, scale, scale2, first, last, heads, live_ref, rows_ref, q_ref, g_ref, stat_ref, *refs):
    n = len(kinds)
    kv, refs = refs[:n], refs[n:]
    if not first:
        dq_in, refs = refs[0], refs[1:]
    dq_ref, outs, accs = refs[0], refs[1:1 + n], refs[1 + n:]
    dh = q_ref.shape[1] // heads
    for acc in accs:
        acc[...] = jnp.zeros_like(acc)

    @pl.loop(0, heads, unroll=2)
    def _(h):
        cols = pl.ds(pl.multiple_of(h * dh, dh), dh)
        q = q_ref[:, cols]
        g = g_ref[:, cols]
        mm = stat_ref[h, 0:1]
        rr = stat_ref[h, 2:3]
        dqt = None if first else dq_in[cols, :]
        for kind, ref, acc in zip(kinds, kv, accs):
            keys = ref[0]
            s = block_scores(kind, keys, q, live_ref, scale2)
            p = jnp.exp2(s - mm)
            dp = dot(ref[1], g, LAST)
            ds = (p * (dp - rr)).astype(jnp.bfloat16)
            acc[1] += dot(p.astype(jnp.bfloat16), g)
            acc[0] += dot(ds, q)
            part = dot(keys.T, ds)
            dqt = part if dqt is None else dqt + part
        if last:
            dq_ref[:, cols] = (dqt.T * scale).astype(dq_ref.dtype)
        else:
            dq_ref[cols, :] = dqt

    for out, acc in zip(outs, accs):
        out[0] = (acc[0] * scale).astype(out.dtype)
        out[1] = acc[1].astype(out.dtype)


def backward(lens, q, g, stats, kinds, blocks, dq, scale, scale2, last):
    rows, width = q.shape
    dh = blocks[0].shape[2]
    heads = width // dh
    first = dq is None
    keys = sum(b.shape[1] for b in blocks)
    if last:
        dq_shape = jax.ShapeDtypeStruct((rows, width), jnp.bfloat16)
    else:
        dq_shape = jax.ShapeDtypeStruct((width, rows), jnp.float32)
    n = 3 + len(blocks) + (not first)
    res = pl.pallas_call(
        functools.partial(backward_kernel, kinds, scale, scale2, first, last, heads),
        in_specs=[SMEM] * 2 + [VMEM] * n,
        out_specs=[VMEM] * (1 + len(blocks)),
        out_shape=[dq_shape] + [jax.ShapeDtypeStruct(b.shape, jnp.bfloat16) for b in blocks],
        scratch_shapes=[pltpu.VMEM(b.shape, jnp.float32) for b in blocks],
        cost_estimate=pl.CostEstimate(flops=10 * heads * rows * keys * dh, bytes_accessed=4 * q.size, transcendentals=heads * rows * keys),
        compiler_params=pltpu.CompilerParams(vmem_limit_bytes=16 * 2**20),
    )(*lens, q, g, stats, *blocks, *([] if first else [dq]))
    return res[0], list(res[1:])


def cut_kernel(keys, prefix_ref, *refs):
    outs, sems = refs[:SPLIT], refs[SPLIT]
    z = lax.axis_index("group") // 2
    copies = []
    for step in (4, 3, 5, 2, 6, 1, 7, 0):
        at = pl.multiple_of(lax.rem(z + step, SPLIT) * keys, keys)
        copies.append(pltpu.make_async_copy(prefix_ref.at[:, pl.ds(at, keys), :], outs[step], sems.at[step]))
    for copy in copies:
        copy.start()
    for copy in copies:
        copy.wait()


def cut(prefix, keys):
    shape = (prefix.shape[0], keys, prefix.shape[2])
    return pl.pallas_call(
        functools.partial(cut_kernel, keys),
        in_specs=[ANY],
        out_specs=[ANY] * SPLIT,
        out_shape=[jax.ShapeDtypeStruct(shape, prefix.dtype)] * SPLIT,
        scratch_shapes=[pltpu.SemaphoreType.DMA((SPLIT,))],
    )(prefix)


def lend_kernel(weight_ref, out_ref, sems):
    core = lax.rem(lax.axis_index("tensor"), 2)
    copies = []
    for at in range(4):
        copies.append(pltpu.make_async_copy(weight_ref.at[:, at, 1 - core], out_ref.at[:, at], sems.at[at]))
        copies[-1].start()
    for copy in copies:
        copy.wait()


def lend(by_core):
    shape = by_core.shape[:2] + by_core.shape[3:]
    return pl.pallas_call(
        lend_kernel,
        in_specs=[ANY],
        out_specs=VMEM,
        out_shape=jax.ShapeDtypeStruct(shape, by_core.dtype),
        scratch_shapes=[pltpu.SemaphoreType.DMA((4,))],
    )(by_core)


def project_kernel(summed_ref, beside_ref, weight_ref, other_ref, out_ref):
    tensor = lax.axis_index("tensor")
    y, core = tensor // 2, lax.rem(tensor, 2)
    for step in range(4):
        at = lax.rem(y + step, 4)
        acc = None
        for j in range(2):
            for rows, block in ((summed_ref[j], weight_ref[j, at, core]), (beside_ref[j], other_ref[j, at])):
                part = dot(rows, block, LAST)
                acc = part if acc is None else acc + part
        out_ref[step] = acc.astype(out_ref.dtype)


def project(summed, beside, by_core, other):
    return pl.pallas_call(
        project_kernel,
        in_specs=[VMEM] * 4,
        out_specs=VMEM,
        out_shape=jax.ShapeDtypeStruct((4, summed.shape[1], by_core.shape[3]), jnp.bfloat16),
        compiler_params=pltpu.CompilerParams(vmem_limit_bytes=16 * 2**20),
    )(summed, beside, by_core, other)


def ring(size, step, stride):
    block = size // stride * stride
    return [(i, (i // stride + step) * stride % block + i % stride) for i in range(size)]


def swap(size):
    return [(i, i ^ 1) for i in range(size)]


def z_hop(x, step):
    return lax.ppermute(x, "group", ring(2 * SPLIT, step, 2))


def x_swap(x):
    return lax.ppermute(x, "group", swap(2 * SPLIT))


def add_low(a, b):
    return (a.astype(jnp.float32) + b.astype(jnp.float32)).astype(jnp.bfloat16)


def on_device(queries, response_kv, grad_out, prefix_kv, kv_weight, resp_len, prefix_len, owner):
    group = lax.axis_index("group")
    z, x = group // 2, group % 2
    dh = prefix_kv.shape[3]
    scale = dh ** (-0.5)
    scale2 = scale * LOG2E
    q, g, own, prefix = queries[0], grad_out[0], response_kv[0], prefix_kv[0]
    lens = (prefix_len, resp_len)
    by_core = kv_weight.reshape(2, 4, 2, kv_weight.shape[1] // 8, dh)

    keys = prefix.shape[1] // SPLIT
    half_way = SPLIT // 2
    owner_z = owner[0] // 2
    away = lax.rem(z - owner_z + SPLIT, SPLIT)

    def branch(holder):
        def body(*pieces):
            got = {}
            for step in (1, 7, 2, 6, 3, 5, 4):
                pairs = [(2 * at + c, 2 * ((at + step) % SPLIT) + c) for at in (holder, holder + half_way) for c in (0, 1)]
                got[step] = lax.ppermute(pieces[step], "group", pairs)
            held = pieces[0]
            for step in range(1, SPLIT):
                held = jnp.where(away == step, got[step], held)
            return held

        return body

    held = lax.switch(lax.rem(owner_z, half_way), [branch(k) for k in range(half_way)], *cut(prefix, keys))
    held, by_core = lax.optimization_barrier((held, by_core))
    swapped, lent = lax.optimization_barrier((x_swap(held), lend(by_core)))
    held = jnp.where(x == owner[0] % 2, held, swapped)

    pieces = {0: held}
    new = [0]
    up = down = held
    stats = None
    other = lax.ppermute(lent, "tensor", swap(8))
    for hop in range(1, half_way + 1):
        up = z_hop(up, 1)
        if hop < half_way:
            down = z_hop(down, -1)
        if hop == 1:
            stats = forward(lens, q, g, (None, 0), [own, held], None, scale2, False)
        else:
            stats = forward(lens, q, g, tuple(new), [pieces[k] for k in new], stats, scale2, False)
        new = [SPLIT - hop]
        if hop < half_way:
            up, down, stats, other = lax.optimization_barrier((up, down, stats, other))
            pieces[hop] = down
            new.append(hop)
        else:
            up, stats = lax.optimization_barrier((up, stats))
        pieces[SPLIT - hop] = up
    stats = forward(lens, q, g, tuple(new), [pieces[k] for k in new], stats, scale2, True)

    dq, (grad,) = backward(lens, q, g, stats, (half_way,), [pieces[half_way]], None, scale, scale2, False)
    up, down = z_hop(grad, 1), None
    for left in range(half_way - 1, 0, -1):
        new = (left, SPLIT - left)
        dq, grads = backward(lens, q, g, stats, new, [pieces[k] for k in new], dq, scale, scale2, False)
        up, dq, *grads = lax.optimization_barrier((up, dq, *grads))
        up = z_hop(add_low(grads[0], up), 1)
        down = z_hop(grads[1] if down is None else add_low(grads[1], down), -1)
    dq, (grad,) = backward(lens, q, g, stats, (0,), [pieces[0]], dq, scale, scale2, False)
    up, down, dq, grad = lax.optimization_barrier((up, down, dq, grad))
    half = keys // 2

    def rows_of(at):
        up_, down_, grad_ = (lax.dynamic_slice_in_dim(v, at * half, half, 1).astype(jnp.float32) for v in (up, down, grad))
        return up_ + down_ + grad_

    swapped = x_swap(rows_of(1 - x).astype(jnp.bfloat16))
    dq, (own_grad,) = backward(lens, q, g, stats, (None,), [own], dq, scale, scale2, True)
    swapped, dq, own_grad = lax.optimization_barrier((swapped, dq, own_grad))
    summed = (rows_of(x) + swapped.astype(jnp.float32)).astype(jnp.bfloat16)

    beside = lax.ppermute(summed, "tensor", swap(8))
    shares = project(summed, beside, by_core, other)
    result = shares[0].astype(jnp.float32)
    for k in (1, 2, 3):
        result = result + lax.ppermute(shares[k], "tensor", ring(8, k, 2)).astype(jnp.float32)
    return dq[None], own_grad[None], result.astype(jnp.bfloat16)


def solution(mesh):
    in_specs = (
        P(("prompt", "group"), None, "tensor"),
        P(("prompt", "group"), None, None, "tensor"),
        P(("prompt", "group"), None, "tensor"),
        P(("prompt", "group"), None, None, "tensor"),
        P(None, None, "tensor"),
        P(("prompt", "group")),
        P("prompt"),
        P("prompt"),
    )
    out_specs = (
        P(("prompt", "group"), None, "tensor"),
        P(("prompt", "group"), None, None, "tensor"),
        P(("prompt", "group"), "tensor"),
    )
    return jax.shard_map(
        on_device, mesh=mesh, in_specs=in_specs, out_specs=out_specs, check_vma=False
    )
```

```python
import functools

import jax
import jax.numpy as jnp
from jax import lax
from jax.experimental import pallas as pl
from jax.experimental.pallas import tpu as pltpu
from jax.sharding import PartitionSpec as P

LAST = (((1,), (1,)), ((), ()))
PLAIN = (((1,), (0,)), ((), ()))
LOG2E = 1.4426950408889634
SPLIT = 8
SMEM = pl.BlockSpec(memory_space=pltpu.SMEM)
VMEM = pl.BlockSpec(memory_space=pltpu.VMEM)
ANY = pl.BlockSpec(memory_space=pl.ANY)


def dot(a, b, dims=PLAIN):
    return lax.dot_general(a, b, dims, preferred_element_type=jnp.float32)


def block_scores(kind, keys, q, live_ref, scale2):
    s = dot(keys, q, LAST) * scale2
    at = lax.broadcasted_iota(jnp.int32, s.shape, 0)
    if kind is None:
        ok = at <= lax.broadcasted_iota(jnp.int32, s.shape, 1)
    else:
        base = lax.rem(lax.axis_index("group") // 2 + kind, SPLIT) * s.shape[0]
        ok = at < live_ref[0] - base
    return jnp.where(ok, s, -jnp.inf)


def forward_kernel(kinds, scale2, first, last, heads, live_ref, rows_ref, q_ref, g_ref, *refs):
    n = len(kinds)
    kv = refs[:n]
    out_ref = refs[-1]
    dh = q_ref.shape[1] // heads

    @pl.loop(0, heads, unroll=2)
    def _(h):
        cols = pl.ds(pl.multiple_of(h * dh, dh), dh)
        q = q_ref[:, cols]
        g = g_ref[:, cols]
        if first:
            m = l = r = None
        else:
            m, l, r = refs[n][h, 0:1], refs[n][h, 1:2], refs[n][h, 2:3]
        for kind, ref in zip(kinds, kv):
            s = block_scores(kind, ref[0], q, live_ref, scale2)
            top = jnp.max(s, 0, keepdims=True)
            new = top if m is None else jnp.maximum(m, top)
            p = jnp.exp2(s - new)
            dp = dot(ref[1], g, LAST)
            lb = jnp.sum(p, 0, keepdims=True)
            rb = jnp.sum(p * dp, 0, keepdims=True)
            if m is None:
                l, r = lb, rb
            else:
                a = jnp.exp2(m - new)
                l, r = l * a + lb, r * a + rb
            m = new
        if last:
            live = lax.broadcasted_iota(jnp.int32, m.shape, 1) < rows_ref[0]
            m = jnp.where(live, m + jnp.log2(l), jnp.inf)
            r = r / l
        out_ref[h, 0:1] = m
        out_ref[h, 1:2] = l
        out_ref[h, 2:3] = r


def forward(lens, q, g, kinds, blocks, stats, scale2, last):
    rows, width = q.shape
    dh = blocks[0].shape[2]
    heads = width // dh
    first = stats is None
    keys = sum(b.shape[1] for b in blocks)
    n = 2 + len(blocks) + (not first)
    return pl.pallas_call(
        functools.partial(forward_kernel, kinds, scale2, first, last, heads),
        in_specs=[SMEM] * 2 + [VMEM] * n,
        out_specs=VMEM,
        out_shape=jax.ShapeDtypeStruct((heads, 8, rows), jnp.float32),
        cost_estimate=pl.CostEstimate(flops=4 * heads * rows * keys * dh, bytes_accessed=4 * q.size, transcendentals=heads * rows * keys),
        compiler_params=pltpu.CompilerParams(vmem_limit_bytes=16 * 2**20),
    )(*lens, q, g, *blocks, *([] if first else [stats]))


def backward_kernel(kinds, scale, scale2, first, last, heads, live_ref, rows_ref, q_ref, g_ref, stat_ref, *refs):
    n = len(kinds)
    kv, refs = refs[:n], refs[n:]
    if not first:
        dq_in, refs = refs[0], refs[1:]
    dq_ref, outs, accs = refs[0], refs[1:1 + n], refs[1 + n:]
    dh = q_ref.shape[1] // heads
    for acc in accs:
        acc[...] = jnp.zeros_like(acc)

    @pl.loop(0, heads, unroll=2)
    def _(h):
        cols = pl.ds(pl.multiple_of(h * dh, dh), dh)
        q = q_ref[:, cols]
        g = g_ref[:, cols]
        mm = stat_ref[h, 0:1]
        rr = stat_ref[h, 2:3]
        dqt = None if first else dq_in[cols, :]
        for kind, ref, acc in zip(kinds, kv, accs):
            keys = ref[0]
            s = block_scores(kind, keys, q, live_ref, scale2)
            p = jnp.exp2(s - mm)
            dp = dot(ref[1], g, LAST)
            ds = (p * (dp - rr)).astype(jnp.bfloat16)
            acc[1] += dot(p.astype(jnp.bfloat16), g)
            acc[0] += dot(ds, q)
            part = dot(keys.T, ds)
            dqt = part if dqt is None else dqt + part
        if last:
            dq_ref[:, cols] = (dqt.T * scale).astype(dq_ref.dtype)
        else:
            dq_ref[cols, :] = dqt

    for out, acc in zip(outs, accs):
        out[0] = (acc[0] * scale).astype(out.dtype)
        out[1] = acc[1].astype(out.dtype)


def backward(lens, q, g, stats, kinds, blocks, dq, scale, scale2, last):
    rows, width = q.shape
    dh = blocks[0].shape[2]
    heads = width // dh
    first = dq is None
    keys = sum(b.shape[1] for b in blocks)
    if last:
        dq_shape = jax.ShapeDtypeStruct((rows, width), jnp.bfloat16)
    else:
        dq_shape = jax.ShapeDtypeStruct((width, rows), jnp.float32)
    n = 3 + len(blocks) + (not first)
    res = pl.pallas_call(
        functools.partial(backward_kernel, kinds, scale, scale2, first, last, heads),
        in_specs=[SMEM] * 2 + [VMEM] * n,
        out_specs=[VMEM] * (1 + len(blocks)),
        out_shape=[dq_shape] + [jax.ShapeDtypeStruct(b.shape, jnp.bfloat16) for b in blocks],
        scratch_shapes=[pltpu.VMEM(b.shape, jnp.float32) for b in blocks],
        cost_estimate=pl.CostEstimate(flops=10 * heads * rows * keys * dh, bytes_accessed=4 * q.size, transcendentals=heads * rows * keys),
        compiler_params=pltpu.CompilerParams(vmem_limit_bytes=16 * 2**20),
    )(*lens, q, g, stats, *blocks, *([] if first else [dq]))
    return res[0], list(res[1:])


def cut_kernel(keys, prefix_ref, *refs):
    outs, sems = refs[:SPLIT], refs[SPLIT]
    z = lax.axis_index("group") // 2
    copies = []
    for step in (4, 3, 5, 2, 6, 1, 7, 0):
        at = pl.multiple_of(lax.rem(z + step, SPLIT) * keys, keys)
        copies.append(pltpu.make_async_copy(prefix_ref.at[:, pl.ds(at, keys), :], outs[step], sems.at[step]))
    for copy in copies:
        copy.start()
    for copy in copies:
        copy.wait()


def cut(prefix, keys):
    shape = (prefix.shape[0], keys, prefix.shape[2])
    return pl.pallas_call(
        functools.partial(cut_kernel, keys),
        in_specs=[ANY],
        out_specs=[ANY] * SPLIT,
        out_shape=[jax.ShapeDtypeStruct(shape, prefix.dtype)] * SPLIT,
        scratch_shapes=[pltpu.SemaphoreType.DMA((SPLIT,))],
    )(prefix)


def lend_kernel(weight_ref, out_ref, sems):
    core = lax.rem(lax.axis_index("tensor"), 2)
    copies = []
    for at in range(4):
        copies.append(pltpu.make_async_copy(weight_ref.at[:, at, 1 - core], out_ref.at[:, at], sems.at[at]))
        copies[-1].start()
    for copy in copies:
        copy.wait()


def lend(by_core):
    shape = by_core.shape[:2] + by_core.shape[3:]
    return pl.pallas_call(
        lend_kernel,
        in_specs=[ANY],
        out_specs=VMEM,
        out_shape=jax.ShapeDtypeStruct(shape, by_core.dtype),
        scratch_shapes=[pltpu.SemaphoreType.DMA((4,))],
    )(by_core)


def project_kernel(summed_ref, beside_ref, weight_ref, other_ref, out_ref):
    tensor = lax.axis_index("tensor")
    y, core = tensor // 2, lax.rem(tensor, 2)
    for step in range(4):
        at = lax.rem(y + step, 4)
        acc = None
        for j in range(2):
            for rows, block in ((summed_ref[j], weight_ref[j, at, core]), (beside_ref[j], other_ref[j, at])):
                part = dot(rows, block, LAST)
                acc = part if acc is None else acc + part
        out_ref[step] = acc.astype(out_ref.dtype)


def project(summed, beside, by_core, other):
    return pl.pallas_call(
        project_kernel,
        in_specs=[VMEM] * 4,
        out_specs=VMEM,
        out_shape=jax.ShapeDtypeStruct((4, summed.shape[1], by_core.shape[3]), jnp.bfloat16),
        compiler_params=pltpu.CompilerParams(vmem_limit_bytes=16 * 2**20),
    )(summed, beside, by_core, other)


def ring(size, step, stride):
    block = size // stride * stride
    return [(i, (i // stride + step) * stride % block + i % stride) for i in range(size)]


def swap(size):
    return [(i, i ^ 1) for i in range(size)]


def z_hop(x, step):
    return lax.ppermute(x, "group", ring(2 * SPLIT, step, 2))


def x_swap(x):
    return lax.ppermute(x, "group", swap(2 * SPLIT))


def add_low(a, b):
    return (a.astype(jnp.float32) + b.astype(jnp.float32)).astype(jnp.bfloat16)


def on_device(queries, response_kv, grad_out, prefix_kv, kv_weight, resp_len, prefix_len, owner):
    group = lax.axis_index("group")
    z, x = group // 2, group % 2
    dh = prefix_kv.shape[3]
    scale = dh ** (-0.5)
    scale2 = scale * LOG2E
    q, g, own, prefix = queries[0], grad_out[0], response_kv[0], prefix_kv[0]
    lens = (prefix_len, resp_len)
    by_core = kv_weight.reshape(2, 4, 2, kv_weight.shape[1] // 8, dh)

    keys = prefix.shape[1] // SPLIT
    half_way = SPLIT // 2
    owner_z = owner[0] // 2
    away = lax.rem(z - owner_z + SPLIT, SPLIT)

    def branch(holder):
        def body(*pieces):
            got = {}
            for step in (1, 7, 2, 6, 3, 5, 4):
                pairs = [(2 * at + c, 2 * ((at + step) % SPLIT) + c) for at in (holder, holder + half_way) for c in (0, 1)]
                got[step] = lax.ppermute(pieces[step], "group", pairs)
            held = pieces[0]
            for step in range(1, SPLIT):
                held = jnp.where(away == step, got[step], held)
            return held

        return body

    held = lax.switch(lax.rem(owner_z, half_way), [branch(k) for k in range(half_way)], *cut(prefix, keys))
    held, by_core = lax.optimization_barrier((held, by_core))
    swapped, lent = lax.optimization_barrier((x_swap(held), lend(by_core)))
    held = jnp.where(x == owner[0] % 2, held, swapped)

    pieces = {0: held}
    new = [0]
    up = down = held
    stats = None
    other = lax.ppermute(lent, "tensor", swap(8))
    for hop in range(1, half_way + 1):
        up = z_hop(up, 1)
        if hop < half_way:
            down = z_hop(down, -1)
        if hop == 1:
            stats = forward(lens, q, g, (None, 0), [own, held], None, scale2, False)
        else:
            stats = forward(lens, q, g, tuple(new), [pieces[k] for k in new], stats, scale2, False)
        new = [SPLIT - hop]
        if hop < half_way:
            up, down, stats, other = lax.optimization_barrier((up, down, stats, other))
            pieces[hop] = down
            new.append(hop)
        else:
            up, stats = lax.optimization_barrier((up, stats))
        pieces[SPLIT - hop] = up
    stats = forward(lens, q, g, tuple(new), [pieces[k] for k in new], stats, scale2, True)

    dq, (grad,) = backward(lens, q, g, stats, (half_way,), [pieces[half_way]], None, scale, scale2, False)
    up, down = z_hop(grad, 1), None
    for left in range(half_way - 1, 0, -1):
        new = (left, SPLIT - left)
        dq, grads = backward(lens, q, g, stats, new, [pieces[k] for k in new], dq, scale, scale2, False)
        up, dq, *grads = lax.optimization_barrier((up, dq, *grads))
        up = z_hop(add_low(grads[0], up), 1)
        down = z_hop(grads[1] if down is None else add_low(grads[1], down), -1)
    dq, (grad,) = backward(lens, q, g, stats, (0,), [pieces[0]], dq, scale, scale2, False)
    up, down, dq, grad = lax.optimization_barrier((up, down, dq, grad))
    half = keys // 2

    def rows_of(at):
        up_, down_, grad_ = (lax.dynamic_slice_in_dim(v, at * half, half, 1).astype(jnp.float32) for v in (up, down, grad))
        return up_ + down_ + grad_

    swapped = x_swap(rows_of(1 - x).astype(jnp.bfloat16))
    dq, (own_grad,) = backward(lens, q, g, stats, (None,), [own], dq, scale, scale2, True)
    swapped, dq, own_grad = lax.optimization_barrier((swapped, dq, own_grad))
    summed = (rows_of(x) + swapped.astype(jnp.float32)).astype(jnp.bfloat16)

    beside = lax.ppermute(summed, "tensor", swap(8))
    shares = project(summed, beside, by_core, other)
    result = shares[0].astype(jnp.float32)
    for k in (2, 3, 1):
        result = result + lax.ppermute(shares[k], "tensor", ring(8, k, 2)).astype(jnp.float32)
    return dq[None], own_grad[None], result.astype(jnp.bfloat16)


def solution(mesh):
    in_specs = (
        P(("prompt", "group"), None, "tensor"),
        P(("prompt", "group"), None, None, "tensor"),
        P(("prompt", "group"), None, "tensor"),
        P(("prompt", "group"), None, None, "tensor"),
        P(None, None, "tensor"),
        P(("prompt", "group")),
        P("prompt"),
        P("prompt"),
    )
    out_specs = (
        P(("prompt", "group"), None, "tensor"),
        P(("prompt", "group"), None, None, "tensor"),
        P(("prompt", "group"), "tensor"),
    )
    return jax.shard_map(
        on_device, mesh=mesh, in_specs=in_specs, out_specs=out_specs, check_vma=False
    )
```
